256 devices in a mesh: seq: 16 (over y, x), tensor: 16 (over z, core).
Axes of the slice: x: 4, y: 4, z: 8, core: 2. Of those that a mesh axis runs over, the one named last changes fastest.
Arguments:
- hidden: bfloat16 [3072, 8192], P('seq', 'tensor'), may hold values from -6 to 6
- d_out: bfloat16 [3072, 8192], P('seq', 'tensor'), may hold values from -6 to 6
- encoded: bfloat16 [80, 128, 896], P('seq'), may hold values from -6 to 6
- w_query: bfloat16 [8192, 4096], P(None, 'tensor'), may hold values from -0.09375 to 0.09375
- w_key: bfloat16 [896, 4096], P(None, 'tensor'), may hold values from -0.1875 to 0.1875
- w_value: bfloat16 [896, 4096], P(None, 'tensor'), may hold values from -1.5 to 1.5
- w_out: bfloat16 [4096, 8192], P('tensor'), may hold values from -0.125 to 0.125
- neighbour_shard: int32 [48, 2], replicated, may hold values from 0 to 15, all different within a row; in each aligned block of 3 rows (0 to 2, 3 to 5, ...) no two rows name the same one
- neighbour_row: int32 [48, 2], replicated, may hold values from 0 to 4
- span_sequence: int32 [48], replicated, may hold values from 0 to 3, never falling along the last dimension, each value on 1 to 24 neighbouring positions
Outputs:
- mixed: bfloat16 [3072, 8192], P('seq', 'tensor')
- d_hidden: bfloat16 [3072, 8192], P('seq', 'tensor')
- d_w_query: float32 [8192, 4096], P('seq', 'tensor')
- d_w_out: float32 [4096, 8192], P('tensor', 'seq')
- d_w_key: float32 [896, 4096], P('seq', 'tensor')
- d_w_value: float32 [896, 4096], P('seq', 'tensor')
- d_encoded: float32 [80, 128, 896], P('seq', 'tensor')
The draws below stay inside these ranges and needn't reach their ends.
Inputs may be any that keep to these rules, and one draw needn't show every extreme that they name: `neighbour_shard`: in each aligned block of 3 spans no shard is named more than 1 times, and in some block one shard is named exactly 1 times; the neighbours of one span lie on different shards; every shard is named by some span. `span_sequence`: never falls from one span to the next; each of the 4 sequences covers 1 to 24 consecutive spans, one exactly 24.
All inputs are finite; a program needn't handle non-finite values.
Results may differ from the reference program's by a relative error of at most 0.023.
Values may be sent and summed in bfloat16 or wider, within the bound.
No kernel may reach another device: no remote copies, remote signals or barrier semaphores. Data moves between devices by JAX's collectives and lax.ppermute only.
A program may use at most 128 MiB of HBM per device.

```python
import math
import jax
import jax.numpy as jnp
import numpy as np
from jax import lax

D = 8192
HEADS = 32
HEAD_DIM = 128
INNER = 4096
ENC = 896
SPAN = 64
NEIGH_LEN = 128
NEIGHBOURS = 2
TOK_DEV = 192
DB_ROWS = 5
SEQ_COUNT = 4
TOKENS = 3072
SPANS_DEV = 3
SPANS = 48
ROWS_ALL = 80
MOST = 1
SEQ_MOST = 24
N_SEQ = 16
N_TENSOR = 16


def set_ends(drawn, key, least, top_value):
    longest = drawn.shape.index(max(drawn.shape))
    spots = []
    for shift in (0, 1):
        where = [jax.random.randint(jax.random.fold_in(key, axis), (), 0, length) for axis, length in enumerate(drawn.shape)]
        where[longest] = (where[longest] + shift) % drawn.shape[longest]
        spots.append(tuple(where))
    return drawn.at[spots[0]].set(least).at[spots[1]].set(top_value)


def spiked(entries, rng, source, target, shards_of, factor):
    def block_of(dim):
        return (jnp.arange(entries.shape[dim]) // (entries.shape[dim] // shards_of)).reshape((-1,) + (1,) * (entries.ndim - 1 - dim))

    first = jax.random.permutation(rng, shards_of)[block_of(target)]
    far = (block_of(target) + shards_of // 2) % shards_of
    return jnp.where((block_of(source) == first) | (block_of(source) == far), factor * entries, entries)


def block_levels(stream_key, extent, shards, least, largest):
    level = 1.0
    for dim, blocks in shards:
        draws = jax.random.uniform(jax.random.fold_in(jax.random.fold_in(stream_key, 6), dim), (blocks,), jnp.float32, least / len(shards), largest / len(shards))
        level = level * jnp.repeat(jnp.exp(draws), extent[dim] // blocks).reshape((-1,) + (1,) * (len(extent) - 1 - dim))
    return level


def profile(amount, total, bound, slope):
    loads = [(1 << 20) // math.isqrt(rank ** slope) + 1 for rank in range(2, amount + 1)]
    rest, given = total - bound - (amount - 1), [1] * (amount - 1)
    while rest > 0:
        candidates = [i for i in range(amount - 1) if given[i] < bound]
        whole, remaining = sum([loads[i] for i in candidates]), rest
        for i in candidates:
            extra = min(bound - given[i], max(1, remaining * loads[i] // whole), rest)
            given[i] = given[i] + extra
            rest = rest - extra
    return np.array([bound] + given)


def uneven_parts(key, number_of, total, most, slope):
    if number_of == 2:
        one = jax.random.randint(key, (), max(1, total - most), min(most, total - 1) + 1)
        return jnp.stack([one, total - one])
    lengths = jnp.asarray(profile(number_of, total, most, slope), jnp.int32)
    twos = (number_of - 1) // 2
    donor, sink = lengths[1:1 + 2 * twos:2], lengths[2:2 + 2 * twos:2]
    room = jnp.minimum(donor - 1, most - sink)
    shifted = jax.random.randint(jax.random.fold_in(key, 1), (twos,), 0, 1 << 20) % (room + 1)
    lengths = lengths.at[1:1 + 2 * twos:2].set(donor - shifted).at[2:2 + 2 * twos:2].set(sink + shifted)
    return lengths[jax.random.permutation(jax.random.fold_in(key, 2), number_of)]


def assign_block(rng, own, number, rows, number_of, top, limit, slope):
    order = jax.random.permutation(rng, number_of)
    packed, usual = shares(number_of, rows * top, limit, slope, True), shares(number_of, rows * top, limit, slope, False)
    places = jnp.arange(number_of)

    def named(sizes, turn):
        used = int((sizes > 0).sum())
        fixed = max(1, used // 4)
        passed = fixed + (places - fixed + turn * (used - fixed)) % max(1, number_of - fixed)
        return jnp.zeros((number_of,), jnp.int32).at[order[jnp.where(places < fixed, places, passed)]].set(jnp.asarray(sizes, jnp.int32))

    sizes = jnp.where(number % 4 == 0, named(packed, number // 4), named(usual, number - number // 4 - 1))
    mixed = jax.random.permutation(jax.random.fold_in(own, 3), number_of)
    giver, sink = mixed[0:number_of // 2 * 2:2], mixed[1:number_of // 2 * 2:2]
    margin = jnp.minimum(sizes[giver] - 1, limit - sizes[sink]) // 2
    margin = jnp.where((giver == order[0]) | (sink == order[0]) | (sizes[sink] == 0), 0, jnp.maximum(margin, 0))
    passed = jax.random.randint(jax.random.fold_in(own, 4), (number_of // 2,), 0, 1 << 20) % (margin + 1)
    sizes = sizes.at[giver].add(-passed).at[sink].add(passed)
    labels = jnp.searchsorted(jnp.cumsum(sizes), jnp.arange(rows * top), side="right").astype(jnp.int32)
    listing = labels.reshape(top, rows).T
    listing = listing[jax.random.permutation(jax.random.fold_in(own, 1), rows)]
    turn = jax.random.randint(jax.random.fold_in(own, 2), (rows, 1), 0, top)
    return jnp.take_along_axis(listing, (jnp.arange(top)[None, :] + turn) % top, axis=1)


def shares(amount, total, bound, skew, full):
    loads = [(1 << 20) // math.isqrt(grade ** skew) + 1 for grade in range(1, amount + 1)]
    largest = bound if full else min(bound, max(-(-total // amount), total * loads[0] // sum(loads)))
    least = 1 if total - largest >= amount - 1 else 0
    holding, surplus = [largest] + [least] * (amount - 1), total - largest - least * (amount - 1)
    while surplus > 0:
        movable = [i for i in range(1, amount) if holding[i] < largest] or [i for i in range(1, amount) if holding[i] < bound]
        mass, left = sum([loads[i] for i in movable]), surplus
        for i in movable:
            extra = min(bound - holding[i], max(1, left * loads[i] // mass), surplus)
            holding[i] = holding[i] + extra
            surplus = surplus - extra
    return np.array(holding)


def gaussian(key, dims, spread, most, shards=(), kind=jnp.bfloat16):
    result = spread * jax.random.normal(key, dims, jnp.float32)
    if shards:
        result = result * block_levels(key, dims, shards, -0.22, 0.18)
    return jnp.clip(result, -most, most).astype(kind)


def bell_draw_with(stream_key, shape, width, bound, split, heavy, held_as=jnp.bfloat16):
    result = width * jax.random.normal(stream_key, shape, jnp.float32)
    if split:
        result = result * block_levels(stream_key, shape, split, -0.22, 0.18)
    return jnp.clip(spiked(result, jax.random.fold_in(stream_key, 3), *heavy), -bound, bound).astype(held_as)


def setup_inputs(seed: int = 0) -> dict:
    keys = jax.random.split(jax.random.key(seed), 11)
    hidden = bell_draw_with(keys[0], (TOKENS, D), 1.0, 6.0, ((0, 16), (1, 16)), (0, 1, 16, 2.0))
    d_out = bell_draw_with(keys[1], (TOKENS, D), 1.0, 6.0, ((0, 16), (1, 16)), (0, 1, 16, 2.0))
    encoded = gaussian(keys[2], (ROWS_ALL, NEIGH_LEN, ENC), 1.0, 6.0, ((0, 16),))
    w_query = bell_draw_with(keys[3], (D, INNER), D ** -0.5, 0.09375, ((1, 16),), (1, 0, 16, 2.0))
    w_key = gaussian(keys[4], (ENC, INNER), ENC ** -0.5, 0.1875, ((1, 16),))
    w_value = gaussian(keys[5], (ENC, INNER), (max(1, ENC // 64)) ** -0.5, 1.5, ((1, 16),))
    w_out = bell_draw_with(keys[6], (INNER, D), INNER ** -0.5, 0.125, ((0, 16),), (0, 1, 16, 2.0))
    neighbour_shard_keys = jax.random.split(jax.random.fold_in(keys[7], 1), SPANS // SPANS_DEV)
    neighbour_shard_turns = jax.random.permutation(jax.random.fold_in(keys[7], 3), SPANS // SPANS_DEV)
    neighbour_shard = jax.vmap(lambda own, number: assign_block(jax.random.fold_in(keys[7], 2), own, number, SPANS_DEV, N_SEQ, NEIGHBOURS, MOST, 2))(neighbour_shard_keys, neighbour_shard_turns).reshape((SPANS, NEIGHBOURS))
    neighbour_row = set_ends(jax.random.randint(keys[8], (SPANS, NEIGHBOURS), 0, DB_ROWS), jax.random.fold_in(keys[8], 1), 0, DB_ROWS - 1).astype(jnp.int32)
    span_sequence = jnp.searchsorted(jnp.cumsum(uneven_parts(keys[9], SEQ_COUNT, SPANS, SEQ_MOST, 0)), jnp.arange(SPANS), side="right").astype(jnp.int32)
    return dict(hidden=hidden, d_out=d_out, encoded=encoded, w_query=w_query, w_key=w_key, w_value=w_value, w_out=w_out, neighbour_shard=neighbour_shard, neighbour_row=neighbour_row, span_sequence=span_sequence)


def rounded(value):
    return lax.optimization_barrier(value.astype(jnp.bfloat16)).astype(jnp.float32)

def grouped_sum(pair_list, part_count):
    stacked = []
    for left_side, right_side in pair_list:
        part_width = left_side.shape[1] // part_count
        left_parts = left_side.reshape(left_side.shape[0], part_count, part_width).transpose(1, 0, 2).astype(jnp.float32)
        right_parts = right_side.reshape(part_count, part_width, right_side.shape[1]).astype(jnp.float32)
        stacked.append((left_parts, right_parts))
    out_rows = pair_list[0][0].shape[0]
    out_cols = pair_list[0][1].shape[1]

    def add_part(running, pieces):
        product = jnp.zeros((out_rows, out_cols), jnp.float32)
        for index in range(len(pieces)):
            product = product + jnp.dot(pieces[index][0], pieces[index][1], precision=lax.Precision.HIGHEST)
        return (running + rounded(product), None)
    running, unused_out = lax.scan(add_part, jnp.zeros((out_rows, out_cols), jnp.float32), stacked)
    return running

def reference(hidden, d_out, encoded, w_query, w_key, w_value, w_out, neighbour_shard, neighbour_row, span_sequence):
    score_scale = 1.0 / math.sqrt(HEAD_DIM)
    spans_dev = TOK_DEV // SPAN
    groups = spans_dev + 1
    all_groups = N_SEQ * groups
    rows_all = N_SEQ * DB_ROWS
    keys_group = NEIGHBOURS * NEIGH_LEN
    enc_rows = encoded.reshape(rows_all * NEIGH_LEN, ENC)
    key_rows = jnp.dot(enc_rows, w_key, preferred_element_type=jnp.float32).astype(jnp.bfloat16).reshape(rows_all, NEIGH_LEN, INNER)
    value_rows = jnp.dot(enc_rows, w_value, preferred_element_type=jnp.float32).astype(jnp.bfloat16).reshape(rows_all, NEIGH_LEN, INNER)
    queries = jnp.dot(hidden, w_query, preferred_element_type=jnp.float32).astype(jnp.bfloat16)
    block_index = jnp.arange(N_SEQ, dtype=jnp.int32)[:, None]
    local_group = jnp.arange(groups, dtype=jnp.int32)[None, :]
    group_span = block_index * spans_dev - 1 + local_group
    live_group = group_span >= 0
    safe_span = jnp.maximum(group_span, 0).astype(jnp.int32)
    row_table = (neighbour_shard * DB_ROWS + neighbour_row).astype(jnp.int32)
    request_rows = row_table[safe_span].reshape(all_groups * NEIGHBOURS)
    live_request = jnp.repeat(live_group.reshape(all_groups), NEIGHBOURS).astype(jnp.float32)
    key_grid = key_rows[request_rows].reshape(all_groups, keys_group, HEADS, HEAD_DIM).astype(jnp.float32)
    value_grid = value_rows[request_rows].reshape(all_groups, keys_group, HEADS, HEAD_DIM).astype(jnp.float32)

    def padded(rows_in):
        blocks = rows_in.reshape(N_SEQ, TOK_DEV, INNER)
        front_pad = jnp.zeros((N_SEQ, 1, INNER), rows_in.dtype)
        back_pad = jnp.zeros((N_SEQ, SPAN - 1, INNER), rows_in.dtype)
        return jnp.concatenate([front_pad, blocks, back_pad], 1).reshape(all_groups, SPAN, HEADS, HEAD_DIM)

    def unpadded(grid_in):
        return grid_in.reshape(N_SEQ, groups * SPAN, INNER)[:, 1:TOK_DEV + 1].reshape(N_SEQ * TOK_DEV, INNER)
    seq_padded = jnp.concatenate([jnp.full((1,), -1, jnp.int32), span_sequence.astype(jnp.int32)])
    group_seq = seq_padded[(block_index * spans_dev + local_group).astype(jnp.int32)]
    position = jnp.arange(groups * SPAN, dtype=jnp.int32).reshape(groups, SPAN)
    exists = (position >= 1) & (position <= TOK_DEV)
    own_span = (block_index[:, :, None] * spans_dev + jnp.clip((position - 1) // SPAN, 0, spans_dev - 1)[None]).astype(jnp.int32)
    valid_rows = exists[None] & (group_seq[:, :, None] == span_sequence[own_span])
    valid_gate = valid_rows.reshape(all_groups, SPAN).astype(jnp.float32)[:, :, None, None]
    query_grid = padded(queries).astype(jnp.float32)
    scores = jnp.einsum('gqhd,gkhd->ghqk', query_grid, key_grid, precision=lax.Precision.HIGHEST) * score_scale
    exp_scores = jnp.exp(scores)
    attn_probs = exp_scores / lax.optimization_barrier(jnp.sum(exp_scores, axis=-1, keepdims=True))
    attn_half = attn_probs.astype(jnp.bfloat16).astype(jnp.float32)
    attended = (jnp.einsum('ghqk,gkhd->gqhd', attn_half, value_grid, precision=lax.Precision.HIGHEST) * valid_gate).astype(jnp.bfloat16)
    attn_rows = unpadded(attended)
    mixed = grouped_sum([(attn_rows, w_out)], N_TENSOR).astype(jnp.bfloat16)
    d_attended = jnp.dot(d_out, w_out.T, preferred_element_type=jnp.float32).astype(jnp.bfloat16)
    d_grid = padded(d_attended).astype(jnp.float32) * valid_gate
    d_probs = jnp.einsum('gqhd,gkhd->ghqk', d_grid, value_grid, precision=lax.Precision.HIGHEST)
    d_scores = (attn_probs * (d_probs - lax.optimization_barrier(jnp.sum(attn_probs * d_probs, axis=-1, keepdims=True))) * score_scale).astype(jnp.bfloat16).astype(jnp.float32)
    d_query = unpadded(jnp.einsum('ghqk,gkhd->gqhd', d_scores, key_grid, precision=lax.Precision.HIGHEST).astype(jnp.bfloat16))
    d_key = jnp.einsum('ghqk,gqhd->gkhd', d_scores, query_grid, precision=lax.Precision.HIGHEST).astype(jnp.bfloat16)
    d_value = jnp.einsum('ghqk,gqhd->gkhd', attn_half, d_grid, precision=lax.Precision.HIGHEST).astype(jnp.bfloat16)
    d_hidden = grouped_sum([(d_query, w_query.T)], N_TENSOR).astype(jnp.bfloat16)
    d_w_query = grouped_sum([(hidden.T, d_query)], N_SEQ)
    d_w_out = grouped_sum([(attn_rows.T, d_out)], N_SEQ)
    key_req = d_key.reshape(all_groups * NEIGHBOURS, NEIGH_LEN, INNER).astype(jnp.float32) * live_request[:, None, None]
    value_req = d_value.reshape(all_groups * NEIGHBOURS, NEIGH_LEN, INNER).astype(jnp.float32) * live_request[:, None, None]
    key_grad = jax.ops.segment_sum(key_req, request_rows, num_segments=rows_all).reshape(rows_all * NEIGH_LEN, INNER).astype(jnp.bfloat16)
    value_grad = jax.ops.segment_sum(value_req, request_rows, num_segments=rows_all).reshape(rows_all * NEIGH_LEN, INNER).astype(jnp.bfloat16)
    d_w_key = grouped_sum([(enc_rows.T, key_grad)], N_SEQ)
    d_w_value = grouped_sum([(enc_rows.T, value_grad)], N_SEQ)
    d_encoded = grouped_sum([(key_grad, w_key.T), (value_grad, w_value.T)], N_TENSOR).reshape(rows_all, NEIGH_LEN, ENC)
    return (mixed, d_hidden, d_w_query, d_w_out, d_w_key, d_w_value, d_encoded)
```

```python
import math

import jax
import jax.numpy as jnp
from jax import lax
from jax.sharding import PartitionSpec as P

HEAD_DIM = 128
ENC = 896
SPAN = 64
NEIGH_LEN = 128
NEIGHBOURS = 2
BF = jnp.bfloat16
F32 = jnp.float32
NZ = 8
NXY = 4


def z_pairs(step):
    return [(2 * z + c, 2 * ((z + step) % NZ) + c) for z in range(NZ) for c in range(2)]


def x_pairs(step):
    return [(y * 4 + x, y * 4 + (x + step) % 4) for y in range(4) for x in range(4)]


def y_pairs(step):
    return [(y * 4 + x, ((y + step) % 4) * 4 + x) for y in range(4) for x in range(4)]


def z_send(value, step):
    return lax.ppermute(value, "tensor", z_pairs(step))


def x_send(value, step):
    return lax.ppermute(value, "seq", x_pairs(step))


def y_send(value, step):
    return lax.ppermute(value, "seq", y_pairs(step))


def sibling(value):
    return lax.ppermute(value, "tensor", [(i, i ^ 1) for i in range(16)])


def z_gather(block):
    half = block.shape[0] // 2
    out = {0: block}
    up = down = block
    for k in range(1, 4):
        up = z_send(up, 1)
        down = z_send(down, -1)
        out[NZ - k] = up
        out[k] = down
    low = z_send(up[:half], 1)
    high = z_send(down[half:], -1)
    out[4] = jnp.concatenate([low, high], 0)
    return [out[k] for k in range(NZ)]


def ring_sum(term, n, send):
    far = n // 2
    last = term(far)
    half = last.shape[0] // 2
    up = send(last[:half].astype(BF), 1)
    down = send(last[half:].astype(BF), -1)
    for k in range(far - 1, 0, -1):
        a = term(k)
        b = term(n - k)
        if k == far - 1:
            a = jnp.concatenate([a[:half] + up.astype(F32), a[half:]], 0)
            b = jnp.concatenate([b[:half], b[half:] + down.astype(F32)], 0)
        else:
            a = a + up.astype(F32)
            b = b + down.astype(F32)
        up = send(a.astype(BF), 1)
        down = send(b.astype(BF), -1)
    return term(0) + up.astype(F32) + down.astype(F32)


def block_tables(neighbour_shard, neighbour_row, seq_blocks, spans_dev):
    per_span = neighbour_shard.shape[1]

    def windows(id_table):
        shifted = jnp.concatenate([jnp.zeros((1, per_span), jnp.int32), id_table], 0)
        current = shifted[1:].reshape(seq_blocks, spans_dev, per_span)
        previous = shifted[:-1].reshape(seq_blocks, spans_dev, per_span)[:, :1]
        return jnp.concatenate([previous, current], 1).reshape(
            seq_blocks, (spans_dev + 1) * per_span
        )

    shards = windows(neighbour_shard)
    row_ids = windows(neighbour_row)
    request_count = (spans_dev + 1) * per_span
    first_block = jnp.arange(seq_blocks)[:, None] == 0
    leading = jnp.arange(request_count)[None, :] < per_span
    live_mask = jnp.logical_not(first_block & leading)
    slot_rank = jnp.broadcast_to(leading.astype(jnp.int32), shards.shape)
    return (shards, row_ids, live_mask, slot_rank)


def body(
    hidden,
    d_out,
    encoded,
    w_query,
    w_key,
    w_value,
    w_out,
    neighbour_shard,
    neighbour_row,
    span_sequence,
):
    seq_blocks = lax.axis_size("seq")
    my_block = lax.axis_index("seq")
    my_part = lax.axis_index("tensor")
    my_y, my_x = my_block // 4, my_block % 4
    my_z, my_core = my_part // 2, my_part % 2
    tok_dev = hidden.shape[0]
    spans_dev = tok_dev // SPAN
    groups = spans_dev + 1
    inner_dev = w_query.shape[1]
    head_dev = inner_dev // HEAD_DIM
    db_rows = encoded.shape[0]
    capacity = 2
    slot_total = seq_blocks * capacity
    requests = groups * NEIGHBOURS
    score_scale = 1.0 / math.sqrt(HEAD_DIM)
    piece = NEIGH_LEN // 16
    feat = hidden.shape[1]
    shards, row_ids, live_mask, slot_rank = block_tables(
        neighbour_shard, neighbour_row, seq_blocks, spans_dev
    )
    serving = (
        live_mask[:, None, :]
        & (shards[:, None, :] == my_block)
        & (slot_rank[:, None, :] == jnp.arange(capacity)[None, :, None])
    )
    slot_row = jnp.sum(jnp.where(serving, row_ids[:, None, :], 0), axis=2).reshape(slot_total)
    slot_used = jnp.any(serving, axis=2).reshape(slot_total)
    picker = ((slot_row[:, None] == jnp.arange(db_rows)[None, :]) & slot_used[:, None]).astype(BF)
    mine_shard = lax.dynamic_index_in_dim(shards, my_block, 0, keepdims=False)
    mine_rank = lax.dynamic_index_in_dim(slot_rank, my_block, 0, keepdims=False)
    mine_live = lax.dynamic_index_in_dim(live_mask, my_block, 0, keepdims=False)
    chooser = (
        ((mine_shard * capacity + mine_rank)[:, None] == jnp.arange(slot_total)[None, :])
        & mine_live[:, None]
    ).astype(BF)

    share = lax.dynamic_slice_in_dim(encoded, my_part * piece, piece, 1)
    outgoing = jnp.einsum("sr,rpc->spc", picker, share, preferred_element_type=F32).astype(BF)
    arrived = lax.all_to_all(
        outgoing.reshape(slot_total * piece, ENC), "seq", split_axis=0, concat_axis=0, tiled=True
    ).reshape(slot_total, piece, ENC)
    enc_piece = jnp.einsum("qs,spc->qpc", chooser, arrived, preferred_element_type=F32).astype(BF)

    hidden_own = jnp.concatenate(z_gather(hidden), 1)
    d_out_own = jnp.concatenate(z_gather(d_out), 1)
    enc_own = jnp.concatenate(z_gather(enc_piece), 1)
    hidden_full = jnp.concatenate([hidden_own, sibling(hidden_own)], 1)
    d_out_full = jnp.concatenate([d_out_own, sibling(d_out_own)], 1)
    enc_rows = jnp.concatenate([enc_own, sibling(enc_own)], 1).reshape(requests * NEIGH_LEN, ENC)

    order = [2 * ((my_z + k) % NZ) + (my_core ^ j) for j in range(2) for k in range(NZ)]
    w_query_rel = jnp.concatenate(
        [lax.dynamic_slice_in_dim(w_query, r * feat, feat, 0) for r in order], 0
    )
    w_out_rel = jnp.concatenate(
        [lax.dynamic_slice_in_dim(w_out, r * feat, feat, 1) for r in order], 1
    )
    key_rows = jnp.dot(enc_rows, w_key, preferred_element_type=F32).astype(BF)
    value_rows = jnp.dot(enc_rows, w_value, preferred_element_type=F32).astype(BF)
    key_block = key_rows.reshape(groups, NEIGHBOURS * NEIGH_LEN, head_dev, HEAD_DIM)
    value_block = value_rows.reshape(groups, NEIGHBOURS * NEIGH_LEN, head_dev, HEAD_DIM)

    seq_padded = jnp.concatenate([jnp.full((1,), -1, jnp.int32), span_sequence])
    group_seq = lax.dynamic_slice_in_dim(seq_padded, my_block * spans_dev, groups)
    own_seq = group_seq[1:]
    position = jnp.arange(groups * SPAN).reshape(groups, SPAN)
    exists = (position >= 1) & (position <= tok_dev)
    own_index = jnp.clip((position - 1) // SPAN, 0, spans_dev - 1)
    token_seq = jnp.sum(
        jnp.where(own_index[:, :, None] == jnp.arange(spans_dev), own_seq, 0), axis=2
    )
    valid_rows = exists & (group_seq[:, None] == token_seq)

    def padded(rows_in):
        front_pad = jnp.zeros((1, inner_dev), rows_in.dtype)
        back_pad = jnp.zeros((SPAN - 1, inner_dev), rows_in.dtype)
        return jnp.concatenate([front_pad, rows_in, back_pad], 0).reshape(
            groups, SPAN, head_dev, HEAD_DIM
        )

    def unpadded(grid_in):
        return grid_in.reshape(groups * SPAN, inner_dev)[1 : tok_dev + 1]

    queries = jnp.dot(hidden_full, w_query_rel, preferred_element_type=F32).astype(BF)
    d_attended = jnp.einsum("td,id->ti", d_out_full, w_out_rel, preferred_element_type=F32)
    d_attended = d_attended.astype(BF)
    query_grid = padded(queries)
    scores = (
        jnp.einsum("gqhd,gkhd->ghqk", query_grid, key_block, preferred_element_type=F32)
        * score_scale
    )
    exp_scores = jnp.exp(scores)
    attn_probs = exp_scores / jnp.sum(exp_scores, axis=-1, keepdims=True)
    attn_half = attn_probs.astype(BF)
    valid_gate = valid_rows.astype(F32)[:, :, None, None]
    attended = (
        jnp.einsum("ghqk,gkhd->gqhd", attn_half, value_block, preferred_element_type=F32)
        * valid_gate
    ).astype(BF)
    attn_rows = unpadded(attended)
    d_grid = padded(d_attended) * valid_rows.astype(BF)[:, :, None, None]
    d_probs = jnp.einsum("gqhd,gkhd->ghqk", d_grid, value_block, preferred_element_type=F32)
    d_scores = (
        attn_probs * (d_probs - jnp.sum(attn_probs * d_probs, axis=-1, keepdims=True)) * score_scale
    ).astype(BF)
    d_query = unpadded(
        jnp.einsum("ghqk,gkhd->gqhd", d_scores, key_block, preferred_element_type=F32).astype(BF)
    )
    d_key = jnp.einsum("ghqk,gqhd->gkhd", d_scores, query_grid, preferred_element_type=F32)
    d_key = d_key.astype(BF).reshape(requests * NEIGH_LEN, inner_dev)
    d_value = jnp.einsum("ghqk,gqhd->gkhd", attn_half, d_grid, preferred_element_type=F32)
    d_value = d_value.astype(BF).reshape(requests * NEIGH_LEN, inner_dev)

    d_enc = jnp.einsum("ri,ci->rc", d_key, w_key, preferred_element_type=F32)
    d_enc = d_enc + jnp.einsum("ri,ci->rc", d_value, w_value, preferred_element_type=F32)
    d_enc = d_enc.astype(BF).reshape(requests, 2, NZ, piece, ENC)
    d_enc_other = sibling(d_enc[:, 1])
    d_enc_sum = ring_sum(
        lambda k: d_enc[:, 0, k].astype(F32) + d_enc_other[:, k].astype(F32), NZ, z_send
    ).astype(BF)
    returning = jnp.einsum("qs,qpc->spc", chooser, d_enc_sum, preferred_element_type=F32)
    returned = lax.all_to_all(
        returning.astype(BF).reshape(slot_total * piece, ENC),
        "seq",
        split_axis=0,
        concat_axis=0,
        tiled=True,
    ).reshape(slot_total, piece, ENC)
    enc_grad = jnp.einsum("sr,spc->rpc", picker, returned, preferred_element_type=F32)

    def feature_sum(partial):
        blocks = partial.astype(BF).reshape(tok_dev, 2, NZ, feat)
        other = sibling(blocks[:, 1])
        return ring_sum(
            lambda k: blocks[:, 0, k].astype(F32) + other[:, k].astype(F32), NZ, z_send
        ).astype(BF)

    def place(dy, dx):
        target = ((my_y + dy) % 4) * 4 + (my_x + dx) % 4
        return (((target % 2) ^ my_core) * NZ + (target // 2 - my_z) % NZ) * feat

    d_wo = jnp.einsum("ti,td->id", attn_rows, d_out_full, preferred_element_type=F32).astype(BF)

    def wo_column(dx):
        return jnp.stack(
            [lax.dynamic_slice_in_dim(d_wo, place(dy, dx), feat, 1) for dy in range(4)], 0
        ).astype(F32)

    wo_half = ring_sum(wo_column, 4, x_send)
    d_w_out = ring_sum(lambda dy: wo_half[dy], 4, y_send)

    mixed = feature_sum(jnp.dot(attn_rows, w_out_rel, preferred_element_type=F32))

    d_wq = jnp.einsum("td,ti->di", hidden_full, d_query, preferred_element_type=F32).astype(BF)
    d_wk = jnp.einsum("rc,ri->ci", enc_rows, d_key, preferred_element_type=F32).astype(BF)
    d_wv = jnp.einsum("rc,ri->ci", enc_rows, d_value, preferred_element_type=F32).astype(BF)
    enc_feat = ENC // seq_blocks

    def wq_block(dy, dx):
        target = ((my_y + dy) % 4) * 4 + (my_x + dx) % 4
        return jnp.concatenate(
            [
                lax.dynamic_slice_in_dim(d_wq, place(dy, dx), feat, 0),
                lax.dynamic_slice_in_dim(d_wk, target * enc_feat, enc_feat, 0),
                lax.dynamic_slice_in_dim(d_wv, target * enc_feat, enc_feat, 0),
            ],
            0,
        )

    wq_half = ring_sum(
        lambda dy: jnp.stack([wq_block(dy, dx) for dx in range(4)], 0).astype(F32), 4, y_send
    )
    wq_sum = ring_sum(lambda dx: wq_half[dx], 4, x_send)

    d_hidden = feature_sum(
        jnp.einsum("ti,di->td", d_query, w_query_rel, preferred_element_type=F32)
    )
    return (
        mixed,
        d_hidden,
        wq_sum[:feat],
        d_w_out,
        wq_sum[feat : feat + enc_feat],
        wq_sum[feat + enc_feat :],
        enc_grad,
    )


def solution(mesh):
    placed = (
        P("seq", "tensor"),
        P("seq", "tensor"),
        P("seq", None, None),
        P(None, "tensor"),
        P(None, "tensor"),
        P(None, "tensor"),
        P("tensor", None),
        P(),
        P(),
        P(),
    )
    return jax.shard_map(
        body,
        mesh=mesh,
        in_specs=placed,
        out_specs=(
            P("seq", "tensor"),
            P("seq", "tensor"),
            P("seq", "tensor"),
            P("tensor", "seq"),
            P("seq", "tensor"),
            P("seq", "tensor"),
            P("seq", "tensor", None),
        ),
        check_vma=False,
    )
```

```python
import math

import jax
import jax.numpy as jnp
from jax import lax
from jax.experimental import pallas as pl
from jax.experimental.pallas import tpu as pltpu
from jax.sharding import PartitionSpec as P

HEAD_DIM = 128
ENC = 896
SPAN = 64
NEIGH_LEN = 128
NEIGHBOURS = 2
BF = jnp.bfloat16
F32 = jnp.float32
NZ = 8
NXY = 4


def z_pairs(step):
    return [(2 * z + c, 2 * ((z + step) % NZ) + c) for z in range(NZ) for c in range(2)]


def x_pairs(step):
    return [(y * 4 + x, y * 4 + (x + step) % 4) for y in range(4) for x in range(4)]


def y_pairs(step):
    return [(y * 4 + x, ((y + step) % 4) * 4 + x) for y in range(4) for x in range(4)]


def z_send(value, step):
    return lax.ppermute(value, "tensor", z_pairs(step))


def x_send(value, step):
    return lax.ppermute(value, "seq", x_pairs(step))


def y_send(value, step):
    return lax.ppermute(value, "seq", y_pairs(step))


def sibling(value):
    return lax.ppermute(value, "tensor", [(i, i ^ 1) for i in range(16)])


NB = 16
VMEM = pl.BlockSpec(memory_space=pltpu.VMEM)
SMEM = pl.BlockSpec(memory_space=pltpu.SMEM)
ANY = pl.BlockSpec(memory_space=pl.ANY)


def call(kernel, out_shape, in_specs, out_specs, scratch, flops, moved, limit=56):
    return pl.pallas_call(
        kernel,
        out_shape=out_shape,
        in_specs=in_specs,
        out_specs=out_specs,
        scratch_shapes=scratch,
        compiler_params=pltpu.CompilerParams(vmem_limit_bytes=limit * 2**20),
        cost_estimate=pl.CostEstimate(flops=0, bytes_accessed=0, transcendentals=0),
    )


def shape(dims, dtype=BF):
    return jax.ShapeDtypeStruct(dims, dtype)


def feature_block(info, r):
    core = info[1] if r < NZ else 1 - info[1]
    return 2 * lax.rem(info[0] + r % NZ, NZ) + core


def contract(a, b, da, db):
    return lax.dot_general(a, b, (((da,), (db,)), ((), ())), preferred_element_type=F32)


def fetch(pairs, sem):
    copies = [pltpu.make_async_copy(src, dst, sem.at[i]) for i, (src, dst) in enumerate(pairs)]
    for copy in copies:
        copy.start()
    return copies


def stack_kernel(far, *refs):
    blocks, out, sem = refs[:-2], refs[-2], refs[-1]
    half = blocks[far].shape[0]
    targets = [out.at[k] for k in range(far)]
    targets += [out.at[far, pl.ds(0, half)], out.at[far, pl.ds(half, half)]]
    targets += [out.at[k] for k in range(far + 1, 2 * far)]
    copies = fetch(list(zip(blocks, targets)), sem)
    for copy in copies:
        copy.wait()


def stacked(blocks):
    rows, columns = blocks[0].shape
    far = (len(blocks) - 1) // 2
    return call(
        lambda *refs: stack_kernel(far, *refs),
        shape((2 * far, rows, columns)),
        [ANY] * len(blocks),
        ANY,
        [pltpu.SemaphoreType.DMA((len(blocks),))],
        0,
        0,
        8,
    )(*blocks)


def rows_kernel(rows, wk, wv, key_out, value_out):
    enc = rows[...].reshape(NB * rows.shape[1], ENC)
    for w, out in ((wk, key_out), (wv, value_out)):
        out[...] = jnp.dot(enc, w[...], preferred_element_type=F32).astype(BF).reshape(out.shape)


def neighbour_rows(enc, w_key, w_value):
    rows, inner = enc.shape[1], w_key.shape[1]
    return call(
        rows_kernel, (shape((NB, rows, inner)),) * 2, [VMEM] * 3, (VMEM, VMEM), [], 0, 0, 24
    )(enc, w_key, w_value)


def half_of(own, other, r):
    return own.at[r] if r < NZ else other.at[r - NZ]


def weight_block(info, w, across, r):
    start = pl.multiple_of(feature_block(info, r) * 512, 512)
    return w.at[:, pl.ds(start, 512)] if across else w.at[pl.ds(start, 512)]


def project_kernel(across, info, own, other, w, out, blocks, held, sem, sem_w):
    got = fetch([(half_of(own, other, r), blocks.at[r]) for r in range(NB)], sem)
    got_w = fetch([(weight_block(info, w, across, r), held.at[r]) for r in range(NB)], sem_w)
    total = None
    for r in range(NB):
        got[r].wait()
        got_w[r].wait()
        term = contract(blocks[r], held[r], 1, 1 if across else 0)
        total = term if total is None else total + term
    out[...] = total.astype(BF)


def project(info, own, other, w, across):
    rows, inner = own.shape[1], w.shape[0 if across else 1]
    return call(
        lambda *refs: project_kernel(across, *refs),
        shape((rows, inner)),
        [SMEM, ANY, ANY, ANY],
        VMEM,
        [
            pltpu.VMEM((NB, rows, 512), BF),
            pltpu.VMEM((NB, inner, 512) if across else (NB, 512, inner), BF),
            pltpu.SemaphoreType.DMA((NB,)),
            pltpu.SemaphoreType.DMA((NB,)),
        ],
        0,
        0,
    )(info, own, other, w)


def attention_kernel(
    queries, d_attended, keys, values, valid, rows_out, dk_out, dv_out
):
    tok, inner = queries.shape
    groups = 4
    scale = 1.0 / math.sqrt(HEAD_DIM)

    def shifted(rows_in):
        wide = jnp.concatenate(
            [rows_in.astype(F32), jnp.zeros((groups * SPAN - tok, inner), F32)], 0
        )
        return pltpu.roll(wide, 1, 0)

    live = valid[...]
    query_pad = shifted(queries[...]).astype(BF)
    grad_pad = (shifted(d_attended[...]) * live).astype(BF)
    att_all, dq_all = [], []
    for g in range(groups):
        at = slice(g * SPAN, (g + 1) * SPAN)
        rows = slice(g * 16, (g + 1) * 16)
        att_heads, dq_heads = [], []
        for h in range(inner // HEAD_DIM):
            col = slice(h * HEAD_DIM, (h + 1) * HEAD_DIM)
            q = query_pad[at, col]
            dg = grad_pad[at, col]
            k = keys[:, rows, col].reshape(NB * 16, HEAD_DIM)
            v = values[:, rows, col].reshape(NB * 16, HEAD_DIM)
            e = jnp.exp(contract(q, k, 1, 1) * scale)
            p = e / jnp.sum(e, axis=-1, keepdims=True)
            half = p.astype(BF)
            att_heads.append(jnp.dot(half, v, preferred_element_type=F32) * live[at])
            dp = contract(dg, v, 1, 1)
            ds = p * (dp - jnp.sum(p * dp, axis=-1, keepdims=True)) * scale
            ds = ds.astype(BF)
            dq_heads.append(jnp.dot(ds, k, preferred_element_type=F32))
            dk = contract(ds, q, 0, 0).astype(BF)
            dv = contract(half, dg, 0, 0).astype(BF)
            dk_out[:, rows, col] = dk.reshape(NB, 16, HEAD_DIM)
            dv_out[:, rows, col] = dv.reshape(NB, 16, HEAD_DIM)
        att_all.append(jnp.concatenate(att_heads, 1))
        dq_all.append(jnp.concatenate(dq_heads, 1))
    last = groups * SPAN - 1
    both = jnp.concatenate([jnp.concatenate(att_all, 0), jnp.concatenate(dq_all, 0)], 1)
    rows_out[...] = pltpu.roll(both, last, 0)[:tok].astype(BF)


def attention(queries, d_attended, keys, values, valid):
    tok, inner = queries.shape
    return call(
        attention_kernel,
        (shape((tok, 2 * inner)),) + (shape(keys.shape),) * 2,
        [VMEM] * 5,
        (VMEM,) * 3,
        [],
        2 * 5 * 256 * 256 * inner,
        3 * 2**20,
        24,
    )(queries, d_attended, keys, values, valid)


def query_weight_kernel(info, rows, own, other, out, blocks, held, sem, sem_out):
    got = fetch([(half_of(own, other, r), blocks.at[r]) for r in range(NB)], sem)
    flipped = rows[:, out.shape[0] :].astype(F32).T.astype(BF)
    copies = []
    for r in range(NB):
        got[r].wait()
        held[r] = jnp.dot(flipped, blocks[r], preferred_element_type=F32).astype(BF)
        start = pl.multiple_of(feature_block(info, r) * 512, 512)
        goal = out.at[:, pl.ds(start, 512)]
        copies.append(pltpu.make_async_copy(held.at[r], goal, sem_out.at[r]))
        copies[-1].start()
    for copy in copies:
        copy.wait()


def query_weight_terms(info, rows, own, other):
    tok, inner = rows.shape[0], rows.shape[1] // 2
    return call(
        query_weight_kernel,
        shape((inner, NB * 512)),
        [SMEM, VMEM, ANY, ANY],
        ANY,
        [pltpu.VMEM((NB, tok, 512), BF), pltpu.VMEM((NB, inner, 512), BF)]
        + [pltpu.SemaphoreType.DMA((NB,))] * 2,
        0,
        0,
    )(info, rows, own, other)


def out_weight_kernel(info, rows, own, other, enc, dk, dv, *refs):
    outs, (blocks, held, side, side_out, sem, sem_out) = refs[:8], refs[8:]
    got = fetch([(half_of(own, other, r), blocks.at[r]) for r in range(NB)], sem)
    inner = held.shape[1]
    flipped = rows[:, :inner].astype(F32).T.astype(BF)
    for copy in got:
        copy.wait()
    copies, targets, goals = [], [], []
    for p in (8, 9, 10, 11, 4, 5, 12, 13, 6, 7, 14, 15, 0, 1, 2, 3):
        dy, dx = p // 4, p % 4
        target = lax.rem(info[2] + dy, 4) * 4 + lax.rem(info[3] + dx, 4)
        far = lax.rem(lax.rem(target, 2) + info[1], 2)
        r = far * NZ + lax.rem(lax.div(target, 2) - info[0] + NZ, NZ)
        targets.append(target)
        goals.append(outs[p // 2].at[p % 2])
        i = len(copies)
        held[i] = jnp.dot(flipped, blocks[r], preferred_element_type=F32).astype(BF)
        goal = goals[i].at[pl.ds(0, inner)]
        copies.append(pltpu.make_async_copy(held.at[i], goal, sem_out.at[i]))
        copies[-1].start()
    count = NB * dk.shape[1]
    both = jnp.concatenate([dk[...].reshape(count, -1), dv[...].reshape(count, -1)], 1)
    side[pl.ds(0, ENC)] = contract(enc[...].reshape(count, ENC), both, 0, 0)
    side[pl.ds(ENC, 64)] = jnp.zeros((64, 512), F32)
    for i in range(NB):
        start = pl.multiple_of(targets[i] * 56, 8)
        side_out[i] = side[pl.ds(start, 64)].astype(BF)
        goal = goals[i].at[pl.ds(inner, 64)]
        copies.append(pltpu.make_async_copy(side_out.at[i], goal, sem_out.at[NB + i]))
        copies[-1].start()
    for copy in copies:
        copy.wait()


def out_weight_terms(info, rows, own, other, enc, dk, dv):
    tok, inner = rows.shape[0], rows.shape[1] // 2
    got = call(
        out_weight_kernel,
        (shape((2, inner + 64, 512)),) * 8,
        [SMEM, VMEM, ANY, ANY, VMEM, VMEM, VMEM],
        (ANY,) * 8,
        [
            pltpu.VMEM((NB, tok, 512), BF),
            pltpu.VMEM((NB, inner, 512), BF),
            pltpu.VMEM((ENC + 64, 512), F32),
            pltpu.VMEM((NB, 64, 512), BF),
            pltpu.SemaphoreType.DMA((NB,)),
            pltpu.SemaphoreType.DMA((2 * NB,)),
        ],
        0,
        0,
    )(info, rows, own, other, enc, dk, dv)
    return [(got[2 * dy], got[2 * dy + 1]) for dy in range(4)]


def enc_kernel(info, dk, dv, wk, wv, own_out, other_out, held, sem):
    half = NZ * dk.shape[1]
    for j in range(2):
        part = pl.ds(j * NZ, NZ)
        grad = contract(dk[part].reshape(half, -1), wk[...], 1, 1)
        grad = grad + contract(dv[part].reshape(half, -1), wv[...], 1, 1)
        held[part] = grad.astype(BF).reshape(NZ, half // NZ, ENC)
    pairs = []
    for r in range(NB):
        goal = own_out.at[r] if r < NZ else other_out.at[r - NZ]
        pairs.append((held.at[feature_block(info, r)], goal))
    for copy in fetch(pairs, sem):
        copy.wait()


def enc_terms(info, dk, dv, wk, wv):
    rows = dk.shape[1]
    return call(
        enc_kernel,
        (shape((NZ, rows, ENC)),) * 2,
        [SMEM] + [VMEM] * 4,
        (ANY, ANY),
        [pltpu.VMEM((NB, rows, ENC), BF), pltpu.SemaphoreType.DMA((NB,))],
        0,
        0,
        24,
    )(info, dk, dv, wk, wv)


def sums_kernel(info, rows, wo, wq, own_out, far_out, near_out, held_o, held_q, held, *sems):
    sem_o, sem_q, sem_out = sems
    order = list(range(NZ, NB)) + list(range(NZ))
    got_o = fetch([(weight_block(info, wo, True, r), held_o.at[r]) for r in order], sem_o)
    got_q = fetch([(weight_block(info, wq, False, r), held_q.at[r]) for r in order], sem_q)
    tok, inner = rows.shape[0], wo.shape[0]
    att, dq = rows[:, :inner], rows[:, inner:]
    outs = []
    for i, r in enumerate(order):
        got_o[i].wait()
        held[r, pl.ds(0, tok)] = jnp.dot(att, held_o[r], preferred_element_type=F32).astype(BF)
        got_q[i].wait()
        held[r, pl.ds(tok, tok)] = contract(dq, held_q[r], 1, 1).astype(BF)
        if r < NZ:
            goal = own_out.at[r]
        elif 3 <= r - NZ <= 5:
            goal = far_out.at[r - NZ - 3]
        else:
            goal = near_out.at[(r - NZ - 6) % NZ]
        outs.append(pltpu.make_async_copy(held.at[r], goal, sem_out.at[r]))
        outs[-1].start()
    for copy in outs:
        copy.wait()


def feature_terms(info, rows, wo, wq):
    tok, inner = rows.shape[0], wo.shape[0]
    height = 2 * tok
    return call(
        sums_kernel,
        (shape((NZ, height, 512)), shape((3, height, 512)), shape((5, height, 512))),
        [SMEM, VMEM, ANY, ANY],
        (ANY, ANY, ANY),
        [
            pltpu.VMEM((NB, inner, 512), BF),
            pltpu.VMEM((NB, 512, inner), BF),
            pltpu.VMEM((NB, height, 512), BF),
            pltpu.SemaphoreType.DMA((NB,)),
            pltpu.SemaphoreType.DMA((NB,)),
            pltpu.SemaphoreType.DMA((NB,)),
        ],
        0,
        0,
    )(info, rows, wo, wq)


def tied(*values):
    return lax.optimization_barrier(values)


def z_both(up, down):
    return z_send(up, 1), z_send(down, -1)


def z_last_by(send, up, down):
    half = up.shape[0] // 2
    return send(up[:half], 1), send(down[half:], -1)


def z_last(up, down):
    return z_last_by(z_send, up, down)


def z_stack(block, one, two, three, four):
    return stacked([block, one[1], two[1], three[1], *four, three[0], two[0], one[0]])


def ring_open(last, send):
    half = last.shape[0] // 2
    return send(last[:half], 1), send(last[half:], -1)


def ring_step(a, b, up, down):
    if up.shape != a.shape:
        half = up.shape[0]
        a = jnp.concatenate([a[:half] + up.astype(F32), a[half:]], 0)
        b = jnp.concatenate([b[:half], b[half:] + down.astype(F32)], 0)
    else:
        a = a + up.astype(F32)
        b = b + down.astype(F32)
    return a.astype(BF), b.astype(BF)


def ring_end(mine, up, down):
    return mine.astype(F32) + up.astype(F32) + down.astype(F32)


def block_tables(neighbour_shard, neighbour_row, seq_blocks, spans_dev):
    per_span = neighbour_shard.shape[1]

    def windows(id_table):
        shifted = jnp.concatenate([jnp.zeros((1, per_span), jnp.int32), id_table], 0)
        current = shifted[1:].reshape(seq_blocks, spans_dev, per_span)
        previous = shifted[:-1].reshape(seq_blocks, spans_dev, per_span)[:, :1]
        return jnp.concatenate([previous, current], 1).reshape(
            seq_blocks, (spans_dev + 1) * per_span
        )

    shards = windows(neighbour_shard)
    row_ids = windows(neighbour_row)
    request_count = (spans_dev + 1) * per_span
    first_block = jnp.arange(seq_blocks)[:, None] == 0
    leading = jnp.arange(request_count)[None, :] < per_span
    live_mask = jnp.logical_not(first_block & leading)
    slot_rank = jnp.broadcast_to(leading.astype(jnp.int32), shards.shape)
    return (shards, row_ids, live_mask, slot_rank)


def body(
    hidden,
    d_out,
    encoded,
    w_query,
    w_key,
    w_value,
    w_out,
    neighbour_shard,
    neighbour_row,
    span_sequence,
):
    seq_blocks = lax.axis_size("seq")
    my_block = lax.axis_index("seq")
    my_part = lax.axis_index("tensor")
    my_y, my_x = my_block // 4, my_block % 4
    my_z, my_core = my_part // 2, my_part % 2
    tok_dev = hidden.shape[0]
    spans_dev = tok_dev // SPAN
    groups = spans_dev + 1
    inner_dev = w_query.shape[1]
    db_rows = encoded.shape[0]
    capacity = 2
    slot_total = seq_blocks * capacity
    requests = groups * NEIGHBOURS
    piece = NEIGH_LEN // 16
    feat = hidden.shape[1]
    shards, row_ids, live_mask, slot_rank = block_tables(
        neighbour_shard, neighbour_row, seq_blocks, spans_dev
    )
    serving = (
        live_mask[:, None, :]
        & (shards[:, None, :] == my_block)
        & (slot_rank[:, None, :] == jnp.arange(capacity)[None, :, None])
    )
    slot_row = jnp.sum(jnp.where(serving, row_ids[:, None, :], 0), axis=2).reshape(slot_total)
    slot_used = jnp.any(serving, axis=2).reshape(slot_total)
    picker = ((slot_row[:, None] == jnp.arange(db_rows)[None, :]) & slot_used[:, None]).astype(BF)
    mine_shard = lax.dynamic_index_in_dim(shards, my_block, 0, keepdims=False)
    mine_rank = lax.dynamic_index_in_dim(slot_rank, my_block, 0, keepdims=False)
    mine_live = lax.dynamic_index_in_dim(live_mask, my_block, 0, keepdims=False)
    chooser = (
        ((mine_shard * capacity + mine_rank)[:, None] == jnp.arange(slot_total)[None, :])
        & mine_live[:, None]
    ).astype(BF)

    share = lax.dynamic_slice_in_dim(encoded, my_part * piece, piece, 1)
    outgoing = jnp.einsum("sr,rpc->spc", picker, share, preferred_element_type=F32).astype(BF)
    info = jnp.stack([my_z, my_core, my_y, my_x]).astype(jnp.int32)
    h1 = z_both(hidden, hidden)
    d1 = z_both(d_out, d_out)
    h1, d1, outgoing = tied(h1, d1, outgoing)
    h2 = z_both(*h1)
    d2 = z_both(*d1)
    arrived = lax.all_to_all(
        outgoing.reshape(slot_total * piece, ENC), "seq", split_axis=0, concat_axis=0, tiled=True
    ).reshape(slot_total, piece, ENC)
    enc_piece = jnp.einsum("qs,spc->qpc", chooser, arrived, preferred_element_type=F32).astype(BF)
    enc_piece = enc_piece.reshape(requests * piece, ENC)
    enc_all = lax.all_gather(enc_piece, "tensor", axis=0)
    h2, d2, enc_piece = tied(h2, d2, enc_piece)
    h3 = z_both(*h2)
    d3 = z_both(*d2)
    h3, d3 = tied(h3, d3)
    h4 = z_last(*h3)
    d4 = z_last(*d3)
    h4, d4 = tied(h4, d4)
    hidden_own = z_stack(hidden, h1, h2, h3, h4)
    hidden_other = sibling(hidden_own)
    d_out_own = z_stack(d_out, d1, d2, d3, d4)
    hidden_other, d_out_own = tied(hidden_other, d_out_own)
    d_out_other = sibling(d_out_own)
    queries = project(info, hidden_own, hidden_other, w_query, False)
    d_out_other, queries = tied(d_out_other, queries)
    d_attended = project(info, d_out_own, d_out_other, w_out, True)

    seq_padded = jnp.concatenate([jnp.full((1,), -1, jnp.int32), span_sequence])
    group_seq = lax.dynamic_slice_in_dim(seq_padded, my_block * spans_dev, groups)
    own_seq = group_seq[1:]
    position = jnp.arange(groups * SPAN).reshape(groups, SPAN)
    exists = (position >= 1) & (position <= tok_dev)
    own_index = jnp.clip((position - 1) // SPAN, 0, spans_dev - 1)
    token_seq = jnp.sum(
        jnp.where(own_index[:, :, None] == jnp.arange(spans_dev), own_seq, 0), axis=2
    )
    valid = (exists & (group_seq[:, None] == token_seq)).astype(F32).reshape(groups * SPAN, 1)

    key_rows, value_rows = neighbour_rows(enc_all, w_key, w_value)
    rows, d_key, d_value = attention(queries, d_attended, key_rows, value_rows, valid)
    d_wo = out_weight_terms(info, rows, d_out_own, d_out_other, enc_all, d_key, d_value)
    d_wo, rows = tied(d_wo, rows)
    yu, yd = y_send(d_wo[2][0], 1), y_send(d_wo[2][1], -1)
    d_wq = query_weight_terms(info, rows, hidden_own, hidden_other)
    d_wq, d_key = tied(d_wq, d_key)
    d_wq = lax.psum_scatter(d_wq, "seq", scatter_dimension=1, tiled=True).astype(F32)
    enc_mine, enc_far = enc_terms(info, d_key, d_value, w_key, w_value)
    enc_mine, enc_far, rows = tied(enc_mine, enc_far, rows)
    enc_got = sibling(enc_far)
    sums_own, sums_far, sums_near = feature_terms(info, rows, w_out, w_query)
    ya = (d_wo[1][0].astype(F32) + yu.astype(F32)).astype(BF)
    yb = (d_wo[3][1].astype(F32) + yd.astype(F32)).astype(BF)
    sums_own, sums_far, sums_near, ya, yb, enc_got = tied(
        sums_own, sums_far, sums_near, ya, yb, enc_got
    )
    got_far = sibling(sums_far)
    got_near = sibling(sums_near)

    def term(k):
        got = got_far[k - 3] if 3 <= k <= 5 else got_near[(k - 6) % NZ]
        return sums_own[k].astype(F32) + got.astype(F32)

    def enc_term(k):
        return enc_mine[k].astype(F32) + enc_got[k].astype(F32)

    y1 = y_send(ya, 1), y_send(yb, -1)
    eu, ed = ring_open(enc_term(4).astype(BF), z_send)
    zu, zd = ring_open(term(4).astype(BF), z_send)
    ea, eb = ring_step(enc_term(3), enc_term(5), eu, ed)
    za, zb = ring_step(term(3), term(5), zu, zd)
    y1, za, zb, ea, eb, got_near = tied(y1, za, zb, ea, eb, got_near)
    y2 = y_send(d_wo[1][1], 1), y_send(d_wo[3][0], -1)
    eu, ed = z_both(ea, eb)
    zu, zd = z_both(za, zb)
    ea, eb = ring_step(enc_term(2), enc_term(6), eu, ed)
    za, zb = ring_step(term(2), term(6), zu, zd)
    y2, za, zb, ea, eb = tied(y2, za, zb, ea, eb)
    eu, ed = z_both(ea, eb)
    zu, zd = z_both(za, zb)
    wo_low = ring_end(d_wo[0][0], y1[0], y2[1])
    wo_high = ring_end(d_wo[0][1], y2[0], y1[1])
    xu, xd = ring_open(wo_high[0].astype(BF), x_send)
    xa, xb = ring_step(wo_low[1], wo_high[1], xu, xd)
    ea, eb = ring_step(enc_term(1), enc_term(7), eu, ed)
    za, zb = ring_step(term(1), term(7), zu, zd)
    za, zb, ea, eb, xa, xb = tied(za, zb, ea, eb, xa, xb)
    eu, ed = z_both(ea, eb)
    zu, zd = z_both(za, zb)
    wo_sum = ring_end(wo_low[0], x_send(xa, 1), x_send(xb, -1))
    d_enc_sum = ring_end(enc_term(0), eu, ed).astype(BF).reshape(requests, piece, ENC)
    grads_sum = ring_end(term(0), zu, zd)
    enc_feat = ENC // seq_blocks

    mixed = grads_sum[:tok_dev].astype(BF)
    returning = jnp.einsum("qs,qpc->spc", chooser, d_enc_sum, preferred_element_type=F32)
    returned = lax.all_to_all(
        returning.astype(BF).reshape(slot_total * piece, ENC),
        "seq",
        split_axis=0,
        concat_axis=0,
        tiled=True,
    ).reshape(slot_total, piece, ENC)
    enc_grad = jnp.einsum("sr,spc->rpc", picker, returned, preferred_element_type=F32)
    return (
        mixed,
        grads_sum[tok_dev:].astype(BF),
        d_wq.T,
        wo_sum[:inner_dev],
        wo_sum[inner_dev : inner_dev + enc_feat, :inner_dev],
        wo_sum[inner_dev : inner_dev + enc_feat, inner_dev:],
        enc_grad,
    )


def solution(mesh):
    placed = (
        P("seq", "tensor"),
        P("seq", "tensor"),
        P("seq", None, None),
        P(None, "tensor"),
        P(None, "tensor"),
        P(None, "tensor"),
        P("tensor", None),
        P(),
        P(),
        P(),
    )
    return jax.shard_map(
        body,
        mesh=mesh,
        in_specs=placed,
        out_specs=(
            P("seq", "tensor"),
            P("seq", "tensor"),
            P("seq", "tensor"),
            P("tensor", "seq"),
            P("seq", "tensor"),
            P("seq", "tensor"),
            P("seq", "tensor", None),
        ),
        check_vma=False,
    )
```

```python
import math

import jax
import jax.numpy as jnp
from jax import lax
from jax.experimental import pallas as pl
from jax.experimental.pallas import tpu as pltpu
from jax.sharding import PartitionSpec as P

HEAD_DIM = 128
ENC = 896
SPAN = 64
NEIGH_LEN = 128
NEIGHBOURS = 2
BF = jnp.bfloat16
F32 = jnp.float32
NZ = 8
NXY = 4


def z_pairs(step):
    return [(2 * z + c, 2 * ((z + step) % NZ) + c) for z in range(NZ) for c in range(2)]


def x_pairs(step):
    return [(y * 4 + x, y * 4 + (x + step) % 4) for y in range(4) for x in range(4)]


def y_pairs(step):
    return [(y * 4 + x, ((y + step) % 4) * 4 + x) for y in range(4) for x in range(4)]


def z_send(value, step):
    return lax.ppermute(value, "tensor", z_pairs(step))


def x_send(value, step):
    return lax.ppermute(value, "seq", x_pairs(step))


def y_send(value, step):
    return lax.ppermute(value, "seq", y_pairs(step))


def sibling(value):
    return lax.ppermute(value, "tensor", [(i, i ^ 1) for i in range(16)])


NB = 16
VMEM = pl.BlockSpec(memory_space=pltpu.VMEM)
SMEM = pl.BlockSpec(memory_space=pltpu.SMEM)
ANY = pl.BlockSpec(memory_space=pl.ANY)


def call(kernel, out_shape, in_specs, out_specs, scratch, flops, moved, limit=56):
    return pl.pallas_call(
        kernel,
        out_shape=out_shape,
        in_specs=in_specs,
        out_specs=out_specs,
        scratch_shapes=scratch,
        compiler_params=pltpu.CompilerParams(vmem_limit_bytes=limit * 2**20),
        cost_estimate=pl.CostEstimate(flops=0, bytes_accessed=0, transcendentals=0),
    )


def shape(dims, dtype=BF):
    return jax.ShapeDtypeStruct(dims, dtype)


def feature_block(info, r):
    core = info[1] if r < NZ else 1 - info[1]
    return 2 * lax.rem(info[0] + r % NZ, NZ) + core


def contract(a, b, da, db):
    return lax.dot_general(a, b, (((da,), (db,)), ((), ())), preferred_element_type=F32)


def fetch(pairs, sem):
    copies = [pltpu.make_async_copy(src, dst, sem.at[i]) for i, (src, dst) in enumerate(pairs)]
    for copy in copies:
        copy.start()
    return copies


def stack_kernel(far, *refs):
    blocks, out, sem = refs[:-2], refs[-2], refs[-1]
    half = blocks[far].shape[0]
    targets = [out.at[k] for k in range(far)]
    targets += [out.at[far, pl.ds(0, half)], out.at[far, pl.ds(half, half)]]
    targets += [out.at[k] for k in range(far + 1, 2 * far)]
    copies = fetch(list(zip(blocks, targets)), sem)
    for copy in copies:
        copy.wait()


def stacked(blocks):
    rows, columns = blocks[0].shape
    far = (len(blocks) - 1) // 2
    return call(
        lambda *refs: stack_kernel(far, *refs),
        shape((2 * far, rows, columns)),
        [ANY] * len(blocks),
        ANY,
        [pltpu.SemaphoreType.DMA((len(blocks),))],
        0,
        0,
        8,
    )(*blocks)


def rows_kernel(rows, wk, wv, key_out, value_out):
    enc = rows[...].reshape(NB * rows.shape[1], ENC)
    for w, out in ((wk, key_out), (wv, value_out)):
        out[...] = jnp.dot(enc, w[...], preferred_element_type=F32).astype(BF).reshape(out.shape)


def neighbour_rows(enc, w_key, w_value):
    rows, inner = enc.shape[1], w_key.shape[1]
    return call(
        rows_kernel, (shape((NB, rows, inner)),) * 2, [VMEM] * 3, (VMEM, VMEM), [], 0, 0, 24
    )(enc, w_key, w_value)


def half_of(own, other, r):
    return own.at[r] if r < NZ else other.at[r - NZ]


def weight_block(info, w, across, r):
    start = pl.multiple_of(feature_block(info, r) * 512, 512)
    return w.at[:, pl.ds(start, 512)] if across else w.at[pl.ds(start, 512)]


def project_kernel(across, info, own, other, w, out, blocks, held, sem, sem_w):
    got = fetch([(half_of(own, other, r), blocks.at[r]) for r in range(NB)], sem)
    got_w = fetch([(weight_block(info, w, across, r), held.at[r]) for r in range(NB)], sem_w)
    total = None
    for r in range(NB):
        got[r].wait()
        got_w[r].wait()
        term = contract(blocks[r], held[r], 1, 1 if across else 0)
        total = term if total is None else total + term
    out[...] = total.astype(BF)


def project(info, own, other, w, across):
    rows, inner = own.shape[1], w.shape[0 if across else 1]
    return call(
        lambda *refs: project_kernel(across, *refs),
        shape((rows, inner)),
        [SMEM, ANY, ANY, ANY],
        VMEM,
        [
            pltpu.VMEM((NB, rows, 512), BF),
            pltpu.VMEM((NB, inner, 512) if across else (NB, 512, inner), BF),
            pltpu.SemaphoreType.DMA((NB,)),
            pltpu.SemaphoreType.DMA((NB,)),
        ],
        0,
        0,
        63,
    )(info, own, other, w)


def attention_kernel(
    queries, d_attended, keys, values, valid, rows_out, dk_out, dv_out
):
    tok, inner = queries.shape
    groups = 4
    scale = 1.0 / math.sqrt(HEAD_DIM)

    def shifted(rows_in):
        wide = jnp.concatenate(
            [rows_in.astype(F32), jnp.zeros((groups * SPAN - tok, inner), F32)], 0
        )
        return pltpu.roll(wide, 1, 0)

    live = valid[...]
    query_pad = shifted(queries[...]).astype(BF)
    grad_pad = (shifted(d_attended[...]) * live).astype(BF)
    att_all, dq_all = [], []
    for g in range(groups):
        at = slice(g * SPAN, (g + 1) * SPAN)
        rows = slice(g * 16, (g + 1) * 16)
        att_heads, dq_heads = [], []
        for h in range(inner // HEAD_DIM):
            col = slice(h * HEAD_DIM, (h + 1) * HEAD_DIM)
            q = query_pad[at, col]
            dg = grad_pad[at, col]
            k = keys[:, rows, col].reshape(NB * 16, HEAD_DIM)
            v = values[:, rows, col].reshape(NB * 16, HEAD_DIM)
            e = jnp.exp(contract(q, k, 1, 1) * scale)
            p = e / jnp.sum(e, axis=-1, keepdims=True)
            half = p.astype(BF)
            att_heads.append(jnp.dot(half, v, preferred_element_type=F32) * live[at])
            dp = contract(dg, v, 1, 1)
            ds = p * (dp - jnp.sum(p * dp, axis=-1, keepdims=True)) * scale
            ds = ds.astype(BF)
            dq_heads.append(jnp.dot(ds, k, preferred_element_type=F32))
            dk = contract(ds, q, 0, 0).astype(BF)
            dv = contract(half, dg, 0, 0).astype(BF)
            dk_out[:, rows, col] = dk.reshape(NB, 16, HEAD_DIM)
            dv_out[:, rows, col] = dv.reshape(NB, 16, HEAD_DIM)
        att_all.append(jnp.concatenate(att_heads, 1))
        dq_all.append(jnp.concatenate(dq_heads, 1))
    last = groups * SPAN - 1
    both = jnp.concatenate([jnp.concatenate(att_all, 0), jnp.concatenate(dq_all, 0)], 1)
    rows_out[...] = pltpu.roll(both, last, 0)[:tok].astype(BF)


def attention(queries, d_attended, keys, values, valid):
    tok, inner = queries.shape
    return call(
        attention_kernel,
        (shape((tok, 2 * inner)),) + (shape(keys.shape),) * 2,
        [VMEM] * 5,
        (VMEM,) * 3,
        [],
        2 * 5 * 256 * 256 * inner,
        3 * 2**20,
        24,
    )(queries, d_attended, keys, values, valid)


def query_weight_kernel(info, rows, own, other, out, blocks, held, sem, sem_out):
    got = fetch([(half_of(own, other, r), blocks.at[r]) for r in range(NB)], sem)
    flipped = rows[:, out.shape[0] :].astype(F32).T.astype(BF)
    copies = []
    for r in range(NB):
        got[r].wait()
        held[r] = jnp.dot(flipped, blocks[r], preferred_element_type=F32).astype(BF)
        start = pl.multiple_of(feature_block(info, r) * 512, 512)
        goal = out.at[:, pl.ds(start, 512)]
        copies.append(pltpu.make_async_copy(held.at[r], goal, sem_out.at[r]))
        copies[-1].start()
    for copy in copies:
        copy.wait()


def query_weight_terms(info, rows, own, other):
    tok, inner = rows.shape[0], rows.shape[1] // 2
    return call(
        query_weight_kernel,
        shape((inner, NB * 512)),
        [SMEM, VMEM, ANY, ANY],
        ANY,
        [pltpu.VMEM((NB, tok, 512), BF), pltpu.VMEM((NB, inner, 512), BF)]
        + [pltpu.SemaphoreType.DMA((NB,))] * 2,
        0,
        0,
    )(info, rows, own, other)


def out_weight_kernel(info, rows, own, other, enc, dk, dv, *refs):
    outs, (blocks, held, side, side_out, sem, sem_out) = refs[:8], refs[8:]
    got = fetch([(half_of(own, other, r), blocks.at[r]) for r in range(NB)], sem)
    inner = held.shape[1]
    flipped = rows[:, :inner].astype(F32).T.astype(BF)
    for copy in got:
        copy.wait()
    copies, targets, goals = [], [], []
    for p in (8, 9, 10, 11, 4, 5, 12, 13, 6, 7, 14, 15, 0, 1, 2, 3):
        dy, dx = p // 4, p % 4
        target = lax.rem(info[2] + dy, 4) * 4 + lax.rem(info[3] + dx, 4)
        far = lax.rem(lax.rem(target, 2) + info[1], 2)
        r = far * NZ + lax.rem(lax.div(target, 2) - info[0] + NZ, NZ)
        targets.append(target)
        goals.append(outs[p // 2].at[p % 2])
        i = len(copies)
        held[i] = jnp.dot(flipped, blocks[r], preferred_element_type=F32).astype(BF)
        goal = goals[i].at[pl.ds(0, inner)]
        copies.append(pltpu.make_async_copy(held.at[i], goal, sem_out.at[i]))
        copies[-1].start()
    count = NB * dk.shape[1]
    both = jnp.concatenate([dk[...].reshape(count, -1), dv[...].reshape(count, -1)], 1)
    side[pl.ds(0, ENC)] = contract(enc[...].reshape(count, ENC), both, 0, 0)
    side[pl.ds(ENC, 64)] = jnp.zeros((64, 512), F32)
    for i in range(NB):
        start = pl.multiple_of(targets[i] * 56, 8)
        side_out[i] = side[pl.ds(start, 64)].astype(BF)
        goal = goals[i].at[pl.ds(inner, 64)]
        copies.append(pltpu.make_async_copy(side_out.at[i], goal, sem_out.at[NB + i]))
        copies[-1].start()
    for copy in copies:
        copy.wait()


def out_weight_terms(info, rows, own, other, enc, dk, dv):
    tok, inner = rows.shape[0], rows.shape[1] // 2
    got = call(
        out_weight_kernel,
        (shape((2, inner + 64, 512)),) * 8,
        [SMEM, VMEM, ANY, ANY, VMEM, VMEM, VMEM],
        (ANY,) * 8,
        [
            pltpu.VMEM((NB, tok, 512), BF),
            pltpu.VMEM((NB, inner, 512), BF),
            pltpu.VMEM((ENC + 64, 512), F32),
            pltpu.VMEM((NB, 64, 512), BF),
            pltpu.SemaphoreType.DMA((NB,)),
            pltpu.SemaphoreType.DMA((2 * NB,)),
        ],
        0,
        0,
    )(info, rows, own, other, enc, dk, dv)
    return [(got[2 * dy], got[2 * dy + 1]) for dy in range(4)]


def enc_kernel(info, dk, dv, wk, wv, own_out, other_out, held, sem):
    half = NZ * dk.shape[1]
    for j in range(2):
        part = pl.ds(j * NZ, NZ)
        grad = contract(dk[part].reshape(half, -1), wk[...], 1, 1)
        grad = grad + contract(dv[part].reshape(half, -1), wv[...], 1, 1)
        held[part] = grad.astype(BF).reshape(NZ, half // NZ, ENC)
    pairs = []
    for r in range(NB):
        goal = own_out.at[r] if r < NZ else other_out.at[r - NZ]
        pairs.append((held.at[feature_block(info, r)], goal))
    for copy in fetch(pairs, sem):
        copy.wait()


def enc_terms(info, dk, dv, wk, wv):
    rows = dk.shape[1]
    return call(
        enc_kernel,
        (shape((NZ, rows, ENC)),) * 2,
        [SMEM] + [VMEM] * 4,
        (ANY, ANY),
        [pltpu.VMEM((NB, rows, ENC), BF), pltpu.SemaphoreType.DMA((NB,))],
        0,
        0,
        24,
    )(info, dk, dv, wk, wv)


def sums_kernel(info, rows, wo, wq, own_out, far_out, near_out, held_o, held_q, held, *sems):
    sem_o, sem_q, sem_out = sems
    order = list(range(NZ, NB)) + list(range(NZ))
    got_o = fetch([(weight_block(info, wo, True, r), held_o.at[r]) for r in order], sem_o)
    got_q = fetch([(weight_block(info, wq, False, r), held_q.at[r]) for r in order], sem_q)
    tok, inner = rows.shape[0], wo.shape[0]
    att, dq = rows[:, :inner], rows[:, inner:]
    outs = []
    for i, r in enumerate(order):
        got_o[i].wait()
        held[r, pl.ds(0, tok)] = jnp.dot(att, held_o[r], preferred_element_type=F32).astype(BF)
        got_q[i].wait()
        held[r, pl.ds(tok, tok)] = contract(dq, held_q[r], 1, 1).astype(BF)
        if r < NZ:
            goal = own_out.at[r]
        elif 3 <= r - NZ <= 5:
            goal = far_out.at[r - NZ - 3]
        else:
            goal = near_out.at[(r - NZ - 6) % NZ]
        outs.append(pltpu.make_async_copy(held.at[r], goal, sem_out.at[r]))
        outs[-1].start()
    for copy in outs:
        copy.wait()


def feature_terms(info, rows, wo, wq):
    tok, inner = rows.shape[0], wo.shape[0]
    height = 2 * tok
    return call(
        sums_kernel,
        (shape((NZ, height, 512)), shape((3, height, 512)), shape((5, height, 512))),
        [SMEM, VMEM, ANY, ANY],
        (ANY, ANY, ANY),
        [
            pltpu.VMEM((NB, inner, 512), BF),
            pltpu.VMEM((NB, 512, inner), BF),
            pltpu.VMEM((NB, height, 512), BF),
            pltpu.SemaphoreType.DMA((NB,)),
            pltpu.SemaphoreType.DMA((NB,)),
            pltpu.SemaphoreType.DMA((NB,)),
        ],
        0,
        0,
    )(info, rows, wo, wq)


def tied(*values):
    return lax.optimization_barrier(values)


def z_both(up, down):
    return z_send(up, 1), z_send(down, -1)


def z_last_by(send, up, down):
    half = up.shape[0] // 2
    return send(up[:half], 1), send(down[half:], -1)


def z_last(up, down):
    return z_last_by(z_send, up, down)


def z_stack(block, one, two, three, four):
    return stacked([block, one[1], two[1], three[1], *four, three[0], two[0], one[0]])


def ring_open(last, send):
    half = last.shape[0] // 2
    return send(last[:half], 1), send(last[half:], -1)


def ring_step(a, b, up, down):
    if up.shape != a.shape:
        half = up.shape[0]
        a = jnp.concatenate([a[:half] + up.astype(F32), a[half:]], 0)
        b = jnp.concatenate([b[:half], b[half:] + down.astype(F32)], 0)
    else:
        a = a + up.astype(F32)
        b = b + down.astype(F32)
    return a.astype(BF), b.astype(BF)


def ring_end(mine, up, down):
    return mine.astype(F32) + up.astype(F32) + down.astype(F32)


def block_tables(neighbour_shard, neighbour_row, seq_blocks, spans_dev):
    per_span = neighbour_shard.shape[1]

    def windows(id_table):
        shifted = jnp.concatenate([jnp.zeros((1, per_span), jnp.int32), id_table], 0)
        current = shifted[1:].reshape(seq_blocks, spans_dev, per_span)
        previous = shifted[:-1].reshape(seq_blocks, spans_dev, per_span)[:, :1]
        return jnp.concatenate([previous, current], 1).reshape(
            seq_blocks, (spans_dev + 1) * per_span
        )

    shards = windows(neighbour_shard)
    row_ids = windows(neighbour_row)
    request_count = (spans_dev + 1) * per_span
    first_block = jnp.arange(seq_blocks)[:, None] == 0
    leading = jnp.arange(request_count)[None, :] < per_span
    live_mask = jnp.logical_not(first_block & leading)
    slot_rank = jnp.broadcast_to(leading.astype(jnp.int32), shards.shape)
    return (shards, row_ids, live_mask, slot_rank)


def body(
    hidden,
    d_out,
    encoded,
    w_query,
    w_key,
    w_value,
    w_out,
    neighbour_shard,
    neighbour_row,
    span_sequence,
):
    seq_blocks = lax.axis_size("seq")
    my_block = lax.axis_index("seq")
    my_part = lax.axis_index("tensor")
    my_y, my_x = my_block // 4, my_block % 4
    my_z, my_core = my_part // 2, my_part % 2
    tok_dev = hidden.shape[0]
    spans_dev = tok_dev // SPAN
    groups = spans_dev + 1
    inner_dev = w_query.shape[1]
    db_rows = encoded.shape[0]
    capacity = 2
    slot_total = seq_blocks * capacity
    requests = groups * NEIGHBOURS
    piece = NEIGH_LEN // 16
    feat = hidden.shape[1]
    shards, row_ids, live_mask, slot_rank = block_tables(
        neighbour_shard, neighbour_row, seq_blocks, spans_dev
    )
    serving = (
        live_mask[:, None, :]
        & (shards[:, None, :] == my_block)
        & (slot_rank[:, None, :] == jnp.arange(capacity)[None, :, None])
    )
    slot_row = jnp.sum(jnp.where(serving, row_ids[:, None, :], 0), axis=2).reshape(slot_total)
    slot_used = jnp.any(serving, axis=2).reshape(slot_total)
    picker = ((slot_row[:, None] == jnp.arange(db_rows)[None, :]) & slot_used[:, None]).astype(BF)
    mine_shard = lax.dynamic_index_in_dim(shards, my_block, 0, keepdims=False)
    mine_rank = lax.dynamic_index_in_dim(slot_rank, my_block, 0, keepdims=False)
    mine_live = lax.dynamic_index_in_dim(live_mask, my_block, 0, keepdims=False)
    chooser = (
        ((mine_shard * capacity + mine_rank)[:, None] == jnp.arange(slot_total)[None, :])
        & mine_live[:, None]
    ).astype(BF)

    share = lax.dynamic_slice_in_dim(encoded, my_part * piece, piece, 1)
    outgoing = jnp.einsum("sr,rpc->spc", picker, share, preferred_element_type=F32).astype(BF)
    info = jnp.stack([my_z, my_core, my_y, my_x]).astype(jnp.int32)
    h1 = z_both(hidden, hidden)
    d1 = z_both(d_out, d_out)
    h1, d1, outgoing = tied(h1, d1, outgoing)
    h2 = z_both(*h1)
    d2 = z_both(*d1)
    arrived = lax.all_to_all(
        outgoing.reshape(slot_total * piece, ENC), "seq", split_axis=0, concat_axis=0, tiled=True
    ).reshape(slot_total, piece, ENC)
    enc_piece = jnp.einsum("qs,spc->qpc", chooser, arrived, preferred_element_type=F32).astype(BF)
    enc_piece = enc_piece.reshape(requests * piece, ENC)
    enc_piece, h2 = tied(enc_piece, h2)
    enc_all = lax.all_gather(enc_piece, "tensor", axis=0)
    h2, d2 = tied(h2, d2)
    h3 = z_both(*h2)
    d3 = z_both(*d2)
    h3, d3 = tied(h3, d3)
    h4 = z_last(*h3)
    d4 = z_last(*d3)
    h4, d4 = tied(h4, d4)
    hidden_own = z_stack(hidden, h1, h2, h3, h4)
    hidden_other = sibling(hidden_own)
    d_out_own = z_stack(d_out, d1, d2, d3, d4)
    hidden_other, d_out_own = tied(hidden_other, d_out_own)
    d_out_other = sibling(d_out_own)
    queries = project(info, hidden_own, hidden_other, w_query, False)
    d_out_other, queries = tied(d_out_other, queries)
    d_attended = project(info, d_out_own, d_out_other, w_out, True)

    seq_padded = jnp.concatenate([jnp.full((1,), -1, jnp.int32), span_sequence])
    group_seq = lax.dynamic_slice_in_dim(seq_padded, my_block * spans_dev, groups)
    own_seq = group_seq[1:]
    position = jnp.arange(groups * SPAN).reshape(groups, SPAN)
    exists = (position >= 1) & (position <= tok_dev)
    own_index = jnp.clip((position - 1) // SPAN, 0, spans_dev - 1)
    token_seq = jnp.sum(
        jnp.where(own_index[:, :, None] == jnp.arange(spans_dev), own_seq, 0), axis=2
    )
    valid = (exists & (group_seq[:, None] == token_seq)).astype(F32).reshape(groups * SPAN, 1)

    key_rows, value_rows = neighbour_rows(enc_all, w_key, w_value)
    rows, d_key, d_value = attention(queries, d_attended, key_rows, value_rows, valid)
    d_wq = query_weight_terms(info, rows, hidden_own, hidden_other)
    d_wq, rows = tied(d_wq, rows)
    d_wq = lax.psum_scatter(d_wq, "seq", scatter_dimension=1, tiled=True).astype(F32)
    d_wo = out_weight_terms(info, rows, d_out_own, d_out_other, enc_all, d_key, d_value)
    d_wo, d_key = tied(d_wo, d_key)
    yu, yd = y_send(d_wo[2][0], 1), y_send(d_wo[2][1], -1)
    enc_mine, enc_far = enc_terms(info, d_key, d_value, w_key, w_value)
    enc_mine, enc_far, rows = tied(enc_mine, enc_far, rows)
    enc_got = sibling(enc_far)
    sums_own, sums_far, sums_near = feature_terms(info, rows, w_out, w_query)
    ya = (d_wo[1][0].astype(F32) + yu.astype(F32)).astype(BF)
    yb = (d_wo[3][1].astype(F32) + yd.astype(F32)).astype(BF)
    def enc_term(k):
        return enc_mine[k].astype(F32) + enc_got[k].astype(F32)

    eu, ed = ring_open(enc_term(4).astype(BF), z_send)
    ea, eb = ring_step(enc_term(3), enc_term(5), eu, ed)
    sums_own, sums_far, sums_near, ya, yb, ea, eb = tied(
        sums_own, sums_far, sums_near, ya, yb, ea, eb
    )
    got_far = sibling(sums_far)
    got_near = sibling(sums_near)

    def term(k):
        got = got_far[k - 3] if 3 <= k <= 5 else got_near[(k - 6) % NZ]
        return sums_own[k].astype(F32) + got.astype(F32)

    y1 = y_send(ya, 1), y_send(yb, -1)
    eu, ed = z_both(ea, eb)
    zu, zd = ring_open(term(4).astype(BF), z_send)
    ea, eb = ring_step(enc_term(2), enc_term(6), eu, ed)
    za, zb = ring_step(term(3), term(5), zu, zd)
    y1, za, zb, ea, eb, got_near = tied(y1, za, zb, ea, eb, got_near)
    y2 = y_send(d_wo[1][1], 1), y_send(d_wo[3][0], -1)
    eu, ed = z_both(ea, eb)
    zu, zd = z_both(za, zb)
    ea, eb = ring_step(enc_term(1), enc_term(7), eu, ed)
    za, zb = ring_step(term(2), term(6), zu, zd)
    y2, za, zb, ea, eb = tied(y2, za, zb, ea, eb)
    eu, ed = z_both(ea, eb)
    zu, zd = z_both(za, zb)
    wo_low = ring_end(d_wo[0][0], y1[0], y2[1])
    wo_high = ring_end(d_wo[0][1], y2[0], y1[1])
    xu, xd = ring_open(wo_high[0].astype(BF), x_send)
    xa, xb = ring_step(wo_low[1], wo_high[1], xu, xd)
    za, zb = ring_step(term(1), term(7), zu, zd)
    d_enc_sum = ring_end(enc_term(0), eu, ed).astype(BF).reshape(requests, piece, ENC)
    returning = jnp.einsum("qs,qpc->spc", chooser, d_enc_sum, preferred_element_type=F32)
    returning = returning.astype(BF).reshape(slot_total * piece, ENC)
    za, zb, returning, xa, xb = tied(za, zb, returning, xa, xb)
    zu, zd = z_both(za, zb)
    wo_sum = ring_end(wo_low[0], x_send(xa, 1), x_send(xb, -1))
    grads_sum = ring_end(term(0), zu, zd)
    enc_feat = ENC // seq_blocks

    mixed = grads_sum[:tok_dev].astype(BF)
    returned = lax.all_to_all(
        returning,
        "seq",
        split_axis=0,
        concat_axis=0,
        tiled=True,
    ).reshape(slot_total, piece, ENC)
    enc_grad = jnp.einsum("sr,spc->rpc", picker, returned, preferred_element_type=F32)
    return (
        mixed,
        grads_sum[tok_dev:].astype(BF),
        d_wq.T,
        wo_sum[:inner_dev],
        wo_sum[inner_dev : inner_dev + enc_feat, :inner_dev],
        wo_sum[inner_dev : inner_dev + enc_feat, inner_dev:],
        enc_grad,
    )


def solution(mesh):
    placed = (
        P("seq", "tensor"),
        P("seq", "tensor"),
        P("seq", None, None),
        P(None, "tensor"),
        P(None, "tensor"),
        P(None, "tensor"),
        P("tensor", None),
        P(),
        P(),
        P(),
    )
    return jax.shard_map(
        body,
        mesh=mesh,
        in_specs=placed,
        out_specs=(
            P("seq", "tensor"),
            P("seq", "tensor"),
            P("seq", "tensor"),
            P("tensor", "seq"),
            P("seq", "tensor"),
            P("seq", "tensor"),
            P("seq", "tensor", None),
        ),
        check_vma=False,
    )
```

```python
import math

import jax
import jax.numpy as jnp
from jax import lax
from jax.experimental import pallas as pl
from jax.experimental.pallas import tpu as pltpu
from jax.sharding import PartitionSpec as P

HEAD_DIM = 128
ENC = 896
SPAN = 64
NEIGH_LEN = 128
NEIGHBOURS = 2
BF = jnp.bfloat16
F32 = jnp.float32
NZ = 8
NXY = 4


def z_pairs(step):
    return [(2 * z + c, 2 * ((z + step) % NZ) + c) for z in range(NZ) for c in range(2)]


def x_pairs(step):
    return [(y * 4 + x, y * 4 + (x + step) % 4) for y in range(4) for x in range(4)]


def y_pairs(step):
    return [(y * 4 + x, ((y + step) % 4) * 4 + x) for y in range(4) for x in range(4)]


def z_send(value, step):
    return lax.ppermute(value, "tensor", z_pairs(step))


def x_send(value, step):
    return lax.ppermute(value, "seq", x_pairs(step))


def y_send(value, step):
    return lax.ppermute(value, "seq", y_pairs(step))


def sibling(value):
    return lax.ppermute(value, "tensor", [(i, i ^ 1) for i in range(16)])


NB = 16
VMEM = pl.BlockSpec(memory_space=pltpu.VMEM)
SMEM = pl.BlockSpec(memory_space=pltpu.SMEM)
ANY = pl.BlockSpec(memory_space=pl.ANY)


def call(kernel, out_shape, in_specs, out_specs, scratch, flops, moved, limit=56):
    return pl.pallas_call(
        kernel,
        out_shape=out_shape,
        in_specs=in_specs,
        out_specs=out_specs,
        scratch_shapes=scratch,
        compiler_params=pltpu.CompilerParams(vmem_limit_bytes=limit * 2**20),
        cost_estimate=pl.CostEstimate(flops=0, bytes_accessed=0, transcendentals=0),
    )


def shape(dims, dtype=BF):
    return jax.ShapeDtypeStruct(dims, dtype)


def feature_block(info, r):
    core = info[1] if r < NZ else 1 - info[1]
    return 2 * lax.rem(info[0] + r % NZ, NZ) + core


def contract(a, b, da, db):
    return lax.dot_general(a, b, (((da,), (db,)), ((), ())), preferred_element_type=F32)


def fetch(pairs, sem):
    copies = [pltpu.make_async_copy(src, dst, sem.at[i]) for i, (src, dst) in enumerate(pairs)]
    for copy in copies:
        copy.start()
    return copies


def stack_kernel(far, *refs):
    blocks, out, sem = refs[:-2], refs[-2], refs[-1]
    half = blocks[far].shape[0]
    targets = [out.at[k] for k in range(far)]
    targets += [out.at[far, pl.ds(0, half)], out.at[far, pl.ds(half, half)]]
    targets += [out.at[k] for k in range(far + 1, 2 * far)]
    copies = fetch(list(zip(blocks, targets)), sem)
    for copy in copies:
        copy.wait()


def stacked(blocks):
    rows, columns = blocks[0].shape
    far = (len(blocks) - 1) // 2
    return call(
        lambda *refs: stack_kernel(far, *refs),
        shape((2 * far, rows, columns)),
        [ANY] * len(blocks),
        ANY,
        [pltpu.SemaphoreType.DMA((len(blocks),))],
        0,
        0,
        8,
    )(*blocks)


def rows_kernel(rows, wk, wv, key_out, value_out):
    enc = rows[...].reshape(NB * rows.shape[1], ENC)
    for w, out in ((wk, key_out), (wv, value_out)):
        out[...] = jnp.dot(enc, w[...], preferred_element_type=F32).astype(BF).reshape(out.shape)


def neighbour_rows(enc, w_key, w_value):
    rows, inner = enc.shape[1], w_key.shape[1]
    return call(
        rows_kernel, (shape((NB, rows, inner)),) * 2, [VMEM] * 3, (VMEM, VMEM), [], 0, 0, 24
    )(enc, w_key, w_value)


def half_of(own, other, r):
    return own.at[r] if r < NZ else other.at[r - NZ]


def weight_block(info, w, across, r):
    start = pl.multiple_of(feature_block(info, r) * 512, 512)
    return w.at[:, pl.ds(start, 512)] if across else w.at[pl.ds(start, 512)]


def project_kernel(across, info, own, other, w, out, blocks, held, sem, sem_w):
    got = fetch([(half_of(own, other, r), blocks.at[r]) for r in range(NB)], sem)
    got_w = fetch([(weight_block(info, w, across, r), held.at[r]) for r in range(NB)], sem_w)
    total = None
    for r in range(NB):
        got[r].wait()
        got_w[r].wait()
        term = contract(blocks[r], held[r], 1, 1 if across else 0)
        total = term if total is None else total + term
    out[...] = total.astype(BF)


def project(info, own, other, w, across):
    rows, inner = own.shape[1], w.shape[0 if across else 1]
    return call(
        lambda *refs: project_kernel(across, *refs),
        shape((rows, inner)),
        [SMEM, ANY, ANY, ANY],
        VMEM,
        [
            pltpu.VMEM((NB, rows, 512), BF),
            pltpu.VMEM((NB, inner, 512) if across else (NB, 512, inner), BF),
            pltpu.SemaphoreType.DMA((NB,)),
            pltpu.SemaphoreType.DMA((NB,)),
        ],
        0,
        0,
        63,
    )(info, own, other, w)


def attention_kernel(
    queries, d_attended, keys, values, valid, rows_out, dk_out, dv_out
):
    tok, inner = queries.shape
    groups = 4
    scale = 1.0 / math.sqrt(HEAD_DIM)

    def shifted(rows_in):
        wide = jnp.concatenate(
            [rows_in.astype(F32), jnp.zeros((groups * SPAN - tok, inner), F32)], 0
        )
        return pltpu.roll(wide, 1, 0)

    live = valid[...]
    query_pad = shifted(queries[...]).astype(BF)
    grad_pad = (shifted(d_attended[...]) * live).astype(BF)
    att_all, dq_all = [], []
    for g in range(groups):
        at = slice(g * SPAN, (g + 1) * SPAN)
        rows = slice(g * 16, (g + 1) * 16)
        att_heads, dq_heads = [], []
        for h in range(inner // HEAD_DIM):
            col = slice(h * HEAD_DIM, (h + 1) * HEAD_DIM)
            q = query_pad[at, col]
            dg = grad_pad[at, col]
            k = keys[:, rows, col].reshape(NB * 16, HEAD_DIM)
            v = values[:, rows, col].reshape(NB * 16, HEAD_DIM)
            e = jnp.exp(contract(q, k, 1, 1) * scale)
            p = e / jnp.sum(e, axis=-1, keepdims=True)
            half = p.astype(BF)
            att_heads.append(jnp.dot(half, v, preferred_element_type=F32) * live[at])
            dp = contract(dg, v, 1, 1)
            ds = p * (dp - jnp.sum(p * dp, axis=-1, keepdims=True)) * scale
            ds = ds.astype(BF)
            dq_heads.append(jnp.dot(ds, k, preferred_element_type=F32))
            dk = contract(ds, q, 0, 0).astype(BF)
            dv = contract(half, dg, 0, 0).astype(BF)
            dk_out[:, rows, col] = dk.reshape(NB, 16, HEAD_DIM)
            dv_out[:, rows, col] = dv.reshape(NB, 16, HEAD_DIM)
        att_all.append(jnp.concatenate(att_heads, 1))
        dq_all.append(jnp.concatenate(dq_heads, 1))
    last = groups * SPAN - 1
    both = jnp.concatenate([jnp.concatenate(att_all, 0), jnp.concatenate(dq_all, 0)], 1)
    rows_out[...] = pltpu.roll(both, last, 0)[:tok].astype(BF)


def attention(queries, d_attended, keys, values, valid):
    tok, inner = queries.shape
    return call(
        attention_kernel,
        (shape((tok, 2 * inner)),) + (shape(keys.shape),) * 2,
        [VMEM] * 5,
        (VMEM,) * 3,
        [],
        2 * 5 * 256 * 256 * inner,
        3 * 2**20,
        24,
    )(queries, d_attended, keys, values, valid)


def query_weight_kernel(info, rows, own, other, out, blocks, held, sem, sem_out):
    got = fetch([(half_of(own, other, r), blocks.at[r]) for r in range(NB)], sem)
    flipped = rows[:, out.shape[0] :].astype(F32).T.astype(BF)
    copies = []
    for r in range(NB):
        got[r].wait()
        held[r] = jnp.dot(flipped, blocks[r], preferred_element_type=F32).astype(BF)
        start = pl.multiple_of(feature_block(info, r) * 512, 512)
        goal = out.at[:, pl.ds(start, 512)]
        copies.append(pltpu.make_async_copy(held.at[r], goal, sem_out.at[r]))
        copies[-1].start()
    for copy in copies:
        copy.wait()


def query_weight_terms(info, rows, own, other):
    tok, inner = rows.shape[0], rows.shape[1] // 2
    return call(
        query_weight_kernel,
        shape((inner, NB * 512)),
        [SMEM, VMEM, ANY, ANY],
        ANY,
        [pltpu.VMEM((NB, tok, 512), BF), pltpu.VMEM((NB, inner, 512), BF)]
        + [pltpu.SemaphoreType.DMA((NB,))] * 2,
        0,
        0,
    )(info, rows, own, other)


def out_weight_kernel(info, rows, own, other, enc, dk, dv, *refs):
    outs, (blocks, held, side, side_out, sem, sem_out) = refs[:8], refs[8:]
    got = fetch([(half_of(own, other, r), blocks.at[r]) for r in range(NB)], sem)
    inner = held.shape[1]
    flipped = rows[:, :inner].astype(F32).T.astype(BF)
    for copy in got:
        copy.wait()
    copies, targets, goals = [], [], []
    for p in (8, 9, 10, 11, 4, 5, 12, 13, 6, 7, 14, 15, 0, 1, 2, 3):
        dy, dx = p // 4, p % 4
        target = lax.rem(info[2] + dy, 4) * 4 + lax.rem(info[3] + dx, 4)
        far = lax.rem(lax.rem(target, 2) + info[1], 2)
        r = far * NZ + lax.rem(lax.div(target, 2) - info[0] + NZ, NZ)
        targets.append(target)
        goals.append(outs[p // 2].at[p % 2])
        i = len(copies)
        held[i] = jnp.dot(flipped, blocks[r], preferred_element_type=F32).astype(BF)
        goal = goals[i].at[pl.ds(0, inner)]
        copies.append(pltpu.make_async_copy(held.at[i], goal, sem_out.at[i]))
        copies[-1].start()
    count = NB * dk.shape[1]
    both = jnp.concatenate([dk[...].reshape(count, -1), dv[...].reshape(count, -1)], 1)
    side[pl.ds(0, ENC)] = contract(enc[...].reshape(count, ENC), both, 0, 0)
    side[pl.ds(ENC, 64)] = jnp.zeros((64, 512), F32)
    for i in range(NB):
        start = pl.multiple_of(targets[i] * 56, 8)
        side_out[i] = side[pl.ds(start, 64)].astype(BF)
        goal = goals[i].at[pl.ds(inner, 64)]
        copies.append(pltpu.make_async_copy(side_out.at[i], goal, sem_out.at[NB + i]))
        copies[-1].start()
    for copy in copies:
        copy.wait()


def out_weight_terms(info, rows, own, other, enc, dk, dv):
    tok, inner = rows.shape[0], rows.shape[1] // 2
    got = call(
        out_weight_kernel,
        (shape((2, inner + 64, 512)),) * 8,
        [SMEM, VMEM, ANY, ANY, VMEM, VMEM, VMEM],
        (ANY,) * 8,
        [
            pltpu.VMEM((NB, tok, 512), BF),
            pltpu.VMEM((NB, inner, 512), BF),
            pltpu.VMEM((ENC + 64, 512), F32),
            pltpu.VMEM((NB, 64, 512), BF),
            pltpu.SemaphoreType.DMA((NB,)),
            pltpu.SemaphoreType.DMA((2 * NB,)),
        ],
        0,
        0,
    )(info, rows, own, other, enc, dk, dv)
    return [(got[2 * dy], got[2 * dy + 1]) for dy in range(4)]


def enc_kernel(info, dk, dv, wk, wv, own_out, other_out, held, sem):
    half = NZ * dk.shape[1]
    for j in range(2):
        part = pl.ds(j * NZ, NZ)
        grad = contract(dk[part].reshape(half, -1), wk[...], 1, 1)
        grad = grad + contract(dv[part].reshape(half, -1), wv[...], 1, 1)
        held[part] = grad.astype(BF).reshape(NZ, half // NZ, ENC)
    pairs = []
    for r in range(NB):
        goal = own_out.at[r] if r < NZ else other_out.at[r - NZ]
        pairs.append((held.at[feature_block(info, r)], goal))
    for copy in fetch(pairs, sem):
        copy.wait()


def enc_terms(info, dk, dv, wk, wv):
    rows = dk.shape[1]
    return call(
        enc_kernel,
        (shape((NZ, rows, ENC)),) * 2,
        [SMEM] + [VMEM] * 4,
        (ANY, ANY),
        [pltpu.VMEM((NB, rows, ENC), BF), pltpu.SemaphoreType.DMA((NB,))],
        0,
        0,
        24,
    )(info, dk, dv, wk, wv)


def sums_kernel(info, rows, wo, wq, own_out, far_out, near_out, held_o, held_q, held, *sems):
    sem_o, sem_q, sem_out = sems
    order = list(range(NZ, NB)) + list(range(NZ))
    got_o = fetch([(weight_block(info, wo, True, r), held_o.at[r]) for r in order], sem_o)
    got_q = fetch([(weight_block(info, wq, False, r), held_q.at[r]) for r in order], sem_q)
    tok, inner = rows.shape[0], wo.shape[0]
    att, dq = rows[:, :inner], rows[:, inner:]
    outs = []
    for i, r in enumerate(order):
        got_o[i].wait()
        held[r, pl.ds(0, tok)] = jnp.dot(att, held_o[r], preferred_element_type=F32).astype(BF)
        got_q[i].wait()
        held[r, pl.ds(tok, tok)] = contract(dq, held_q[r], 1, 1).astype(BF)
        if r < NZ:
            goal = own_out.at[r]
        elif 3 <= r - NZ <= 5:
            goal = far_out.at[r - NZ - 3]
        else:
            goal = near_out.at[(r - NZ - 6) % NZ]
        outs.append(pltpu.make_async_copy(held.at[r], goal, sem_out.at[r]))
        outs[-1].start()
    for copy in outs:
        copy.wait()


def feature_terms(info, rows, wo, wq):
    tok, inner = rows.shape[0], wo.shape[0]
    height = 2 * tok
    return call(
        sums_kernel,
        (shape((NZ, height, 512)), shape((3, height, 512)), shape((5, height, 512))),
        [SMEM, VMEM, ANY, ANY],
        (ANY, ANY, ANY),
        [
            pltpu.VMEM((NB, inner, 512), BF),
            pltpu.VMEM((NB, 512, inner), BF),
            pltpu.VMEM((NB, height, 512), BF),
            pltpu.SemaphoreType.DMA((NB,)),
            pltpu.SemaphoreType.DMA((NB,)),
            pltpu.SemaphoreType.DMA((NB,)),
        ],
        0,
        0,
    )(info, rows, wo, wq)


def tied(*values):
    return lax.optimization_barrier(values)


def z_both(up, down):
    return z_send(up, 1), z_send(down, -1)


def z_last_by(send, up, down):
    half = up.shape[0] // 2
    return send(up[:half], 1), send(down[half:], -1)


def z_last(up, down):
    return z_last_by(z_send, up, down)


def z_stack(block, one, two, three, four):
    return stacked([block, one[1], two[1], three[1], *four, three[0], two[0], one[0]])


def ring_open(last, send):
    half = last.shape[0] // 2
    return send(last[:half], 1), send(last[half:], -1)


def ring_step(a, b, up, down):
    if up.shape != a.shape:
        half = up.shape[0]
        a = jnp.concatenate([a[:half] + up.astype(F32), a[half:]], 0)
        b = jnp.concatenate([b[:half], b[half:] + down.astype(F32)], 0)
    else:
        a = a + up.astype(F32)
        b = b + down.astype(F32)
    return a.astype(BF), b.astype(BF)


def ring_end(mine, up, down):
    return mine.astype(F32) + up.astype(F32) + down.astype(F32)


def block_tables(neighbour_shard, neighbour_row, seq_blocks, spans_dev):
    per_span = neighbour_shard.shape[1]

    def windows(id_table):
        shifted = jnp.concatenate([jnp.zeros((1, per_span), jnp.int32), id_table], 0)
        current = shifted[1:].reshape(seq_blocks, spans_dev, per_span)
        previous = shifted[:-1].reshape(seq_blocks, spans_dev, per_span)[:, :1]
        return jnp.concatenate([previous, current], 1).reshape(
            seq_blocks, (spans_dev + 1) * per_span
        )

    shards = windows(neighbour_shard)
    row_ids = windows(neighbour_row)
    request_count = (spans_dev + 1) * per_span
    first_block = jnp.arange(seq_blocks)[:, None] == 0
    leading = jnp.arange(request_count)[None, :] < per_span
    live_mask = jnp.logical_not(first_block & leading)
    slot_rank = jnp.broadcast_to(leading.astype(jnp.int32), shards.shape)
    return (shards, row_ids, live_mask, slot_rank)


def body(
    hidden,
    d_out,
    encoded,
    w_query,
    w_key,
    w_value,
    w_out,
    neighbour_shard,
    neighbour_row,
    span_sequence,
):
    seq_blocks = lax.axis_size("seq")
    my_block = lax.axis_index("seq")
    my_part = lax.axis_index("tensor")
    my_y, my_x = my_block // 4, my_block % 4
    my_z, my_core = my_part // 2, my_part % 2
    tok_dev = hidden.shape[0]
    spans_dev = tok_dev // SPAN
    groups = spans_dev + 1
    inner_dev = w_query.shape[1]
    db_rows = encoded.shape[0]
    capacity = 2
    slot_total = seq_blocks * capacity
    requests = groups * NEIGHBOURS
    piece = NEIGH_LEN // 16
    feat = hidden.shape[1]
    shards, row_ids, live_mask, slot_rank = block_tables(
        neighbour_shard, neighbour_row, seq_blocks, spans_dev
    )
    serving = (
        live_mask[:, None, :]
        & (shards[:, None, :] == my_block)
        & (slot_rank[:, None, :] == jnp.arange(capacity)[None, :, None])
    )
    slot_row = jnp.sum(jnp.where(serving, row_ids[:, None, :], 0), axis=2).reshape(slot_total)
    slot_used = jnp.any(serving, axis=2).reshape(slot_total)
    picker = ((slot_row[:, None] == jnp.arange(db_rows)[None, :]) & slot_used[:, None]).astype(BF)
    mine_shard = lax.dynamic_index_in_dim(shards, my_block, 0, keepdims=False)
    mine_rank = lax.dynamic_index_in_dim(slot_rank, my_block, 0, keepdims=False)
    mine_live = lax.dynamic_index_in_dim(live_mask, my_block, 0, keepdims=False)
    chooser = (
        ((mine_shard * capacity + mine_rank)[:, None] == jnp.arange(slot_total)[None, :])
        & mine_live[:, None]
    ).astype(BF)

    share = lax.dynamic_slice_in_dim(encoded, my_part * piece, piece, 1)
    outgoing = jnp.einsum("sr,rpc->spc", picker, share, preferred_element_type=F32).astype(BF)
    info = jnp.stack([my_z, my_core, my_y, my_x]).astype(jnp.int32)
    h1 = z_both(hidden, hidden)
    d1 = z_both(d_out, d_out)
    h1, d1, outgoing = tied(h1, d1, outgoing)
    h2 = z_both(*h1)
    d2 = z_both(*d1)
    arrived = lax.all_to_all(
        outgoing.reshape(slot_total * piece, ENC), "seq", split_axis=0, concat_axis=0, tiled=True
    ).reshape(slot_total, piece, ENC)
    enc_piece = jnp.einsum("qs,spc->qpc", chooser, arrived, preferred_element_type=F32).astype(BF)
    enc_piece = enc_piece.reshape(requests * piece, ENC)
    enc_piece, h2 = tied(enc_piece, h2)
    enc_all = lax.all_gather(enc_piece, "tensor", axis=0)
    h2, d2 = tied(h2, d2)
    h3 = z_both(*h2)
    d3 = z_both(*d2)
    h3, d3 = tied(h3, d3)
    h4 = z_last(*h3)
    d4 = z_last(*d3)
    h4, d4 = tied(h4, d4)
    hidden_own = z_stack(hidden, h1, h2, h3, h4)
    hidden_other = sibling(hidden_own)
    d_out_own = z_stack(d_out, d1, d2, d3, d4)
    hidden_other, d_out_own = tied(hidden_other, d_out_own)
    d_out_other = sibling(d_out_own)
    queries = project(info, hidden_own, hidden_other, w_query, False)
    d_out_other, queries = tied(d_out_other, queries)
    d_attended = project(info, d_out_own, d_out_other, w_out, True)

    seq_padded = jnp.concatenate([jnp.full((1,), -1, jnp.int32), span_sequence])
    group_seq = lax.dynamic_slice_in_dim(seq_padded, my_block * spans_dev, groups)
    own_seq = group_seq[1:]
    position = jnp.arange(groups * SPAN).reshape(groups, SPAN)
    exists = (position >= 1) & (position <= tok_dev)
    own_index = jnp.clip((position - 1) // SPAN, 0, spans_dev - 1)
    token_seq = jnp.sum(
        jnp.where(own_index[:, :, None] == jnp.arange(spans_dev), own_seq, 0), axis=2
    )
    valid = (exists & (group_seq[:, None] == token_seq)).astype(F32).reshape(groups * SPAN, 1)

    key_rows, value_rows = neighbour_rows(enc_all, w_key, w_value)
    rows, d_key, d_value = attention(queries, d_attended, key_rows, value_rows, valid)
    d_wq = query_weight_terms(info, rows, hidden_own, hidden_other)
    d_wq, rows = tied(d_wq, rows)
    d_wq = lax.psum_scatter(d_wq, "seq", scatter_dimension=1, tiled=True).astype(F32)
    d_wo = out_weight_terms(info, rows, d_out_own, d_out_other, enc_all, d_key, d_value)
    d_wo, d_key = tied(d_wo, d_key)
    yu, yd = y_send(d_wo[2][0], 1), y_send(d_wo[2][1], -1)
    enc_mine, enc_far = enc_terms(info, d_key, d_value, w_key, w_value)
    enc_mine, enc_far, rows = tied(enc_mine, enc_far, rows)
    enc_got = sibling(enc_far)
    sums_own, sums_far, sums_near = feature_terms(info, rows, w_out, w_query)
    ya = (d_wo[1][0].astype(F32) + yu.astype(F32)).astype(BF)
    yb = (d_wo[3][1].astype(F32) + yd.astype(F32)).astype(BF)
    def enc_term(k):
        return enc_mine[k].astype(F32) + enc_got[k].astype(F32)

    eu, ed = ring_open(enc_term(4).astype(BF), z_send)
    ea, eb = ring_step(enc_term(3), enc_term(5), eu, ed)
    sums_own, sums_far, sums_near, ya, yb, ea, eb = tied(
        sums_own, sums_far, sums_near, ya, yb, ea, eb
    )
    got_far = sibling(sums_far)
    got_near = sibling(sums_near)

    def term(k):
        got = got_far[k - 3] if 3 <= k <= 5 else got_near[(k - 6) % NZ]
        return sums_own[k].astype(F32) + got.astype(F32)

    y1 = y_send(ya, 1), y_send(yb, -1)
    eu, ed = z_both(ea, eb)
    zu, zd = ring_open(term(4).astype(BF), z_send)
    ea, eb = ring_step(enc_term(2), enc_term(6), eu, ed)
    za, zb = ring_step(term(3), term(5), zu, zd)
    y1, za, zb, ea, eb, got_near = tied(y1, za, zb, ea, eb, got_near)
    y2 = y_send(d_wo[1][1], 1), y_send(d_wo[3][0], -1)
    eu, ed = z_both(ea, eb)
    zu, zd = z_both(za, zb)
    ea, eb = ring_step(enc_term(1), enc_term(7), eu, ed)
    za, zb = ring_step(term(2), term(6), zu, zd)
    y2, za, zb, ea, eb = tied(y2, za, zb, ea, eb)
    eu, ed = z_both(ea, eb)
    zu, zd = z_both(za, zb)
    wo_low = ring_end(d_wo[0][0], y1[0], y2[1])
    wo_high = ring_end(d_wo[0][1], y2[0], y1[1])
    xu, xd = ring_open(wo_high[0].astype(BF), x_send)
    xa, xb = ring_step(wo_low[1], wo_high[1], xu, xd)
    za, zb = ring_step(term(1), term(7), zu, zd)
    d_enc_sum = ring_end(enc_term(0), eu, ed).astype(BF).reshape(requests, piece, ENC)
    returning = jnp.einsum("qs,qpc->spc", chooser, d_enc_sum, preferred_element_type=F32)
    returning = returning.astype(BF).reshape(slot_total * piece, ENC)
    za, zb, returning, xa, xb = tied(za, zb, returning, xa, xb)
    zu, zd = z_both(za, zb)
    wo_sum = ring_end(wo_low[0], x_send(xa, 1), x_send(xb, -1))
    zu, zd, d_w_query = tied(zu, zd, d_wq.T)
    grads_sum = ring_end(term(0), zu, zd)
    enc_feat = ENC // seq_blocks

    mixed = grads_sum[:tok_dev].astype(BF)
    returned = lax.all_to_all(
        returning,
        "seq",
        split_axis=0,
        concat_axis=0,
        tiled=True,
    ).reshape(slot_total, piece, ENC)
    enc_grad = jnp.einsum("sr,spc->rpc", picker, returned, preferred_element_type=F32)
    return (
        mixed,
        grads_sum[tok_dev:].astype(BF),
        d_w_query,
        wo_sum[:inner_dev],
        wo_sum[inner_dev : inner_dev + enc_feat, :inner_dev],
        wo_sum[inner_dev : inner_dev + enc_feat, inner_dev:],
        enc_grad,
    )


def solution(mesh):
    placed = (
        P("seq", "tensor"),
        P("seq", "tensor"),
        P("seq", None, None),
        P(None, "tensor"),
        P(None, "tensor"),
        P(None, "tensor"),
        P("tensor", None),
        P(),
        P(),
        P(),
    )
    return jax.shard_map(
        body,
        mesh=mesh,
        in_specs=placed,
        out_specs=(
            P("seq", "tensor"),
            P("seq", "tensor"),
            P("seq", "tensor"),
            P("tensor", "seq"),
            P("seq", "tensor"),
            P("seq", "tensor"),
            P("seq", "tensor", None),
        ),
        check_vma=False,
    )
```
